32 devices in a mesh: row: 8 (over y, x, core), col: 4 (over z).
Axes of the slice: x: 2, y: 2, z: 4, core: 2. Of those that a mesh axis runs over, the one named last changes fastest.
Arguments:
- hidden: bfloat16 [1792, 8192], P('col', 'row'), may hold values from -6 to 6
- down_weight: bfloat16 [8192, 4096], P('row', 'col'), may hold values from -0.0625 to 0.0625
- tokens: bfloat16 [1792, 4096], P(None, 'col'), may hold values from -6 to 6
- layer_scale: bfloat16 [4096], P('col'), may hold values from 0.25 to 1
- merge_weight: bfloat16 [4, 4096, 4096], P(None, 'col', 'row'), may hold values from -0.046875 to 0.046875
- text_embeds: bfloat16 [2048, 4096], P('col', 'row'), may hold values from -6 to 6
- positions: int32 [448], replicated, may hold values from 0 to 2047, as said below
Outputs:
- prompt_states: bfloat16 [2048, 4096], P('col', 'row')
The draws below stay inside these ranges and needn't reach their ends.
Inputs may be any that keep to these rules, and one draw needn't show every extreme that they name: All distinct; the merged rows of each of 28 pictures occupy consecutive positions in their own order, the pictures appear in the prompt in any order, and position 0 holds an image row.
All inputs are finite; a program needn't handle non-finite values.
Results may differ from the reference program's by a relative error of at most 0.0034.
Values may be sent and summed in bfloat16 or wider, within the bound.
No kernel may reach another device: no remote copies, remote signals or barrier semaphores. Data moves between devices by JAX's collectives and lax.ppermute only.
A program may use at most 64 MiB of HBM per device.

```python
import jax
import jax.numpy as jnp

D = 4096
FF = 8192
DEC = 4096
PATCHES = 1792
MERGED = 448
PROMPT = 2048
PICS = 28


def draw_positions(key, part):
    text_count = PROMPT - MERGED
    middle = MERGED // 2
    cut_key, order_key, text_key = jax.random.split(jax.random.fold_in(key, 17), 3)
    others = jax.random.permutation(cut_key, MERGED - 2)[:PICS - 2].astype(jnp.int32) + 1
    others = others + (others >= middle).astype(jnp.int32)
    cut_points = jnp.sort(jnp.concatenate([others, jnp.array([middle], dtype=jnp.int32)]))
    firsts = jnp.concatenate([jnp.zeros((1,), jnp.int32), cut_points])
    lasts = jnp.concatenate([cut_points, jnp.array([MERGED], dtype=jnp.int32)])
    pic_sizes = lasts - firsts
    starred = jnp.sum((cut_points <= middle).astype(jnp.int32))
    shuffled = jax.random.permutation(order_key, PICS).astype(jnp.int32)
    slot_index = jnp.arange(PICS, dtype=jnp.int32)
    star_slot = jnp.sum(jnp.where(shuffled == starred, slot_index, 0))
    order = jnp.where(slot_index == 0, starred, jnp.where(slot_index == star_slot, shuffled[0], shuffled))
    gaps = jnp.sort(jax.random.randint(text_key, (PICS,), 0, text_count + 1).astype(jnp.int32))
    gaps = jnp.where(slot_index == 0, 0, gaps)
    ordered_sizes = pic_sizes[order]
    slot_start = jnp.cumsum(ordered_sizes) - ordered_sizes + gaps
    rank = jnp.zeros((PICS,), jnp.int32).at[order].set(slot_index)
    pic_start = slot_start[rank]
    merged_rows = jnp.arange(MERGED, dtype=jnp.int32)
    picture = jnp.sum((merged_rows[:, None] >= cut_points[None, :]).astype(jnp.int32), axis=1)
    return (pic_start[picture] + merged_rows - firsts[picture]).astype(jnp.int32)


def levels(key, dims, pieces, low, largest):
    def one(axis_at, shards_of):
        steps = jax.random.uniform(jax.random.fold_in(jax.random.fold_in(key, 6), axis_at), (shards_of,), jnp.float32, low / len(pieces), largest / len(pieces))
        return jnp.repeat(jnp.exp(steps), dims[axis_at] // shards_of).reshape((-1,) + (1,) * (len(dims) - axis_at - 1))

    gain = one(*pieces[0])
    for cut in pieces[1:]:
        gain = gain * one(*cut)
    return gain


def scatter_about(stream_key, shape, width, most, pieces=(), kind=jnp.bfloat16):
    result = jax.random.normal(stream_key, shape, jnp.float32) * width
    if len(pieces) > 0:
        result = levels(stream_key, shape, pieces, -0.22, 0.18) * result
    return jnp.clip(result, min=-most, max=most).astype(kind)


def setup_inputs(seed: int = 0) -> dict:
    key_list = jax.random.split(jax.random.key(seed), 8)
    return {
        "hidden": scatter_about(key_list[0], (PATCHES, FF), 1.0, 6.0, ((0, 4), (1, 8))),
        "down_weight": scatter_about(key_list[1], (FF, D), FF ** -0.5, 0.0625, ((0, 8), (1, 4))),
        "tokens": scatter_about(key_list[2], (PATCHES, D), 1.0, 6.0, ((1, 4),)),
        "layer_scale": jnp.clip(0.25 + 0.75 * jax.random.uniform(key_list[3], (D,), jnp.float32) ** levels(key_list[3], (D,), ((0, 4),), -0.2, 0.2), 0.25, 1.0).astype(jnp.bfloat16),
        "merge_weight": scatter_about(key_list[4], (4, D, DEC), (4 * D) ** -0.5, 0.046875, ((1, 4), (2, 8))),
        "text_embeds": scatter_about(key_list[5], (PROMPT, DEC), 1.0, 6.0, ((0, 4), (1, 8))),
        "positions": draw_positions(jax.random.fold_in(key_list[7], 71), 0),
    }


def reference(hidden, down_weight, tokens, layer_scale, merge_weight, text_embeds, positions):
    down = jnp.dot(hidden, down_weight, preferred_element_type=jnp.float32)
    vision = (tokens.astype(jnp.float32) + layer_scale.astype(jnp.float32)[None, :] * down).astype(jnp.bfloat16)
    merged = vision.reshape(MERGED, 4 * D)
    projected = jnp.dot(merged, merge_weight.reshape(4 * D, DEC), preferred_element_type=jnp.float32).astype(jnp.bfloat16)
    return text_embeds.at[positions.astype(jnp.int32)].set(projected)
```

```python
import functools

import jax
import jax.numpy as jnp
from jax import lax
from jax.experimental import pallas as pl
from jax.experimental.pallas import tpu as pltpu
from jax.sharding import PartitionSpec as P

BF = jnp.bfloat16
F32 = jnp.float32
ANY = pl.BlockSpec(memory_space=pl.ANY)
LITTLE = pl.CostEstimate(flops=1, bytes_accessed=1, transcendentals=0)
ROOM = 8 * 1024 * 1024


def _dot(a, b):
    return jnp.dot(a, b, preferred_element_type=F32)


def _down_kernel(half, blocks, info, *refs):
    w, give, keep = refs[blocks], refs[-2], refs[-1]
    mine = info[0]
    block = refs[0][...] if blocks == 1 else jnp.where(info[1] > 0, refs[0][...], refs[1][...])
    give[...] = _dot(block, w[:, pl.ds(pl.multiple_of((1 - mine) * half, half), half)]).astype(BF)
    keep[...] = _dot(block, w[:, pl.ds(pl.multiple_of(mine * half, half), half)])


def _add_kernel(mine, came, *refs):
    refs[-1][...] = (mine[...].astype(F32) + came[...].astype(F32)).astype(refs[-1].dtype)


def _sum_kernel(mine, came, *refs):
    total = mine[...] + came[...].astype(F32)
    refs[-2][...] = total.astype(BF)
    refs[-1][...] = total


def _vision_kernel(mine, came, tokens, scale, *refs):
    out, spread = refs[-2], refs[-1]
    for j in range(spread.shape[0]):
        lanes = pl.ds(j * 128, 128)
        total = mine[:, lanes].astype(F32) + came[:, lanes].astype(F32)
        vision = tokens[:, lanes].astype(F32) + scale[:, lanes].astype(F32) * total
        spread[j] = vision.astype(BF).astype(F32)
        for k in range(4):
            out[k, :, lanes] = spread[j, pl.ds(k, out.shape[1], stride=4), :].astype(BF)


def _merge_kernel(half, info, own, other, weight, *refs):
    give, total, held, sems = refs[-4:]
    mine = info[0]
    copies = [pltpu.make_async_copy(weight.at[k], held.at[k], sems.at[k]) for k in range(4)]
    for copy in copies:
        copy.start()
    here = pl.ds(pl.multiple_of(mine * half, half), half)
    there = pl.ds(pl.multiple_of((1 - mine) * half, half), half)
    part = None
    for k in range(4):
        copies[k].wait()
        more = _dot(own[k], held[k, here, :]) + _dot(other[k], held[k, there, :])
        part = more if part is None else part + more
    total[...] = part
    give[...] = part.astype(BF)


HBM = pl.BlockSpec(memory_space=pltpu.HBM)
VMEM = pl.BlockSpec(memory_space=pltpu.VMEM)
SMEM = pl.BlockSpec(memory_space=pltpu.SMEM)


def build(rows, cols):
    def swap(x, axis, bit):
        size = rows if axis == "row" else cols
        return lax.ppermute(x, axis, [(i, i ^ bit) for i in range(size)])

    def per_device(hidden, down_weight, tokens, layer_scale, merge_weight, text_embeds, positions):
        patches, depth = hidden.shape
        width = down_weight.shape[1]
        half = width // 2
        merged_rows = patches // 4
        dec = merge_weight.shape[2]
        row, col = lax.axis_index("row"), lax.axis_index("col")
        mine = row % 2
        inner = (col == 1) | (col == 2)
        info = jnp.stack([mine, inner.astype(jnp.int32)])
        scale = lax.dynamic_slice(layer_scale, (mine * half,), (half,))[None, :]
        row_bits = [1 << i for i in range(1, rows.bit_length() - 1)]
        after = []

        def down(*blocks):
            count = blocks[0].shape[0]
            give, keep = pl.pallas_call(
                functools.partial(_down_kernel, half, len(blocks)),
                out_shape=(
                    jax.ShapeDtypeStruct((count, half), BF),
                    jax.ShapeDtypeStruct((count, half), F32),
                ),
                in_specs=[SMEM] + [VMEM] * (len(blocks) + 1) + [ANY] * len(after),
                out_specs=(VMEM, VMEM),
                cost_estimate=LITTLE,
                compiler_params=pltpu.CompilerParams(vmem_limit_bytes=ROOM),
                name="down",
            )(info, *blocks, down_weight, *after)
            after[:] = [give]
            return give, keep

        def add(total, came):
            give = pl.pallas_call(
                _add_kernel,
                out_shape=jax.ShapeDtypeStruct(total.shape, BF),
                in_specs=[VMEM, VMEM] + [ANY] * len(after),
                out_specs=VMEM,
                cost_estimate=LITTLE,
                compiler_params=pltpu.CompilerParams(vmem_limit_bytes=ROOM),
                name="add",
            )(total, came, *after)
            after[:] = [give]
            return give

        def add_both(total, came):
            give, total = pl.pallas_call(
                _sum_kernel,
                out_shape=(
                    jax.ShapeDtypeStruct(total.shape, BF),
                    jax.ShapeDtypeStruct(total.shape, F32),
                ),
                in_specs=[VMEM, VMEM] + [ANY] * len(after),
                out_specs=(VMEM, VMEM),
                cost_estimate=LITTLE,
                compiler_params=pltpu.CompilerParams(vmem_limit_bytes=ROOM),
                name="add_both",
            )(total, came, *after)
            after[:] = [give]
            return give, total

        def see(total, came, first):
            count = total.shape[0]
            residual = lax.dynamic_slice(tokens, (first, mine * half), (count, half))
            out = pl.pallas_call(
                _vision_kernel,
                out_shape=jax.ShapeDtypeStruct((4, count // 4, half), BF),
                in_specs=[VMEM] * 4 + [ANY] * len(after),
                out_specs=VMEM,
                scratch_shapes=[pltpu.VMEM((half // 128, count, 128), F32)],
                cost_estimate=LITTLE,
                compiler_params=pltpu.CompilerParams(vmem_limit_bytes=ROOM),
                name="vision",
            )(total, came, residual, scale, *after)
            after[:] = [out]
            return out

        def merge(own, other):
            count = own.shape[1]
            give, total = pl.pallas_call(
                functools.partial(_merge_kernel, half),
                out_shape=(
                    jax.ShapeDtypeStruct((count, dec), BF),
                    jax.ShapeDtypeStruct((count, dec), F32),
                ),
                in_specs=[SMEM, VMEM, VMEM, HBM] + [ANY] * len(after),
                out_specs=(VMEM, VMEM),
                scratch_shapes=[pltpu.VMEM(merge_weight.shape, BF), pltpu.SemaphoreType.DMA((4,))],
                cost_estimate=LITTLE,
                compiler_params=pltpu.CompilerParams(vmem_limit_bytes=ROOM),
                name="merge",
            )(info, own, other, merge_weight, *after)
            after[:] = [give]
            return give, total

        def place(projected, where_to):
            prompt_count = text_embeds.shape[0]
            prompt_index = col * prompt_count + jnp.arange(prompt_count, dtype=jnp.int32)
            hit = where_to[None, :] == prompt_index[:, None]
            image_rows = _dot(hit.astype(BF), projected).astype(BF)
            return jnp.where(jnp.any(hit, axis=1)[:, None], image_rows, text_embeds)

        if cols != 4:
            parts = jnp.zeros((cols * merged_rows, dec), F32)
            for step in range(cols):
                block = hidden if step == 0 else swap(hidden, "col", step)
                owner = jnp.bitwise_xor(col, step)
                give, total = down(block)
                came = swap(give, "row", 1)
                for bit in row_bits:
                    total = add(total, came)
                    came = swap(total, "row", bit)
                own = see(total, came, owner * patches)
                _, part = merge(own, swap(own, "row", 1))
                parts = lax.dynamic_update_slice(parts, part, (owner * merged_rows, 0))
            return place(lax.psum(parts, "col").astype(BF), positions)

        low = col < 2
        between, outward = [(1, 2), (2, 1)], [(1, 0), (2, 3)]
        near, far = jnp.where(low, 2, 1), jnp.where(low, 3, 0)
        bit_x, bit_y = (row_bits + row_bits)[:2] if row_bits else (1, 1)

        hop_a = swap(hidden, "col", 1)
        hop_b = lax.ppermute(hidden, "col", between)
        hop_c = lax.ppermute(hop_b, "col", outward)
        hop_d = lax.ppermute(hop_a, "col", between)
        rest = patches - patches // 4 // 64 * 64 - 64
        hop_e = [lax.ppermute(hop_d[:rest], "col", outward), lax.ppermute(hop_d[rest:], "col", outward)]

        def x(give):
            return swap(give, "row", bit_x)

        def y(give):
            return swap(give, "row", bit_y)

        def core(give):
            return swap(give, "row", 1)

        def pairs(give):
            return swap(give, "col", 1)

        def halves(give):
            return swap(give, "col", 2)

        even = col % 2 == 0

        def ordered(a, b):
            return jnp.concatenate([jnp.where(even, a, b), jnp.where(even, b, a)], axis=0)

        g0, k0 = down(hidden)
        c0 = core(g0)
        a0 = add(k0, c0)
        x0 = x(a0)
        g1, k1 = down(hop_a)
        c1 = core(g1)
        b0 = add(a0, x0)
        y0 = y(b0)
        a1 = add(k1, c1)
        x1 = x(a1)
        g2, k2 = down(hop_b, hop_c)
        c2 = core(g2)
        b1 = add(a1, x1)
        y1 = y(b1)
        v0 = see(b0, y0, col * patches)
        o0 = core(v0)
        a2 = add(k2, c2)
        x2 = x(a2)
        s0, p0 = merge(v0, o0)
        v1 = see(b1, y1, (col ^ 1) * patches)
        o1 = core(v1)
        g3, k3 = down(hop_d[:rest], hop_e[0])
        c3 = core(g3)
        b2 = add(a2, x2)
        y2 = y(b2)
        a3 = add(k3, c3)
        x3 = x(a3)
        s1, p1 = merge(v1, o1)
        z01 = pairs(ordered(s0, s1))
        g4, k4 = down(hop_d[rest:], hop_e[1])
        c4 = core(g4)
        v2 = see(b2, y2, near * patches)
        o2 = core(v2)
        b3 = add(a3, x3)
        y3 = y(b3)
        a4 = add(k4, c4)
        x4 = x(a4)
        s2, p2 = merge(v2, o2)
        z2 = pairs(s2)
        b4 = add(a4, x4)
        y4 = y(b4)
        give, p01 = add_both(ordered(p0, p1), z01)
        far01 = halves(give)
        v3 = see(b3, y3, far * patches)
        o3 = core(v3)
        give, p2 = add_both(p2, z2)
        far2 = halves(give)
        v4 = see(b4, y4, far * patches + rest)
        o4 = core(v4)
        s3, p3 = merge(v3, o3)
        z3 = pairs(s3)
        s4, p4 = merge(v4, o4)
        z4 = pairs(s4)
        give, p3 = add_both(p3, z3)
        far3 = halves(give)
        give, p4 = add_both(p4, z4)
        far4 = halves(give)
        pair, far_pair, far_p2 = p01, far01, far2
        p3 = jnp.concatenate([p3, p4], axis=0)
        far_p3 = jnp.concatenate([far3, far4], axis=0)

        far_pair, far_p2, far_p3 = far_pair.astype(F32), far_p2.astype(F32), far_p3.astype(F32)
        first, second = pair[:merged_rows], pair[merged_rows:]
        f_first, f_second = far_pair[:merged_rows], far_pair[merged_rows:]
        own_inner = jnp.where(low, second, first) + far_p2
        own_outer = jnp.where(low, first, second) + far_p3
        away_inner = p2 + jnp.where(low, f_first, f_second)
        away_outer = p3 + jnp.where(low, f_second, f_first)
        projected = jnp.concatenate([own_inner, own_outer, away_inner, away_outer], axis=0).astype(BF)
        at = [positions[i * merged_rows : (i + 1) * merged_rows] for i in range(4)]
        where_to = jnp.concatenate(
            [
                jnp.where(low, at[1], at[2]),
                jnp.where(low, at[0], at[3]),
                jnp.where(low, at[2], at[1]),
                jnp.where(low, at[3], at[0]),
            ]
        )
        return place(projected, where_to)

    return per_device


def solution(mesh):
    in_specs = (
        P("col", "row"),
        P("row", "col"),
        P(None, "col"),
        P("col"),
        P(None, "col", "row"),
        P("col", "row"),
        P(),
    )
    out_specs = P("col", "row")
    return jax.shard_map(
        build(mesh.shape["row"], mesh.shape["col"]),
        mesh=mesh,
        in_specs=in_specs,
        out_specs=out_specs,
        check_vma=False,
    )
```

```python
import functools

import jax
import jax.numpy as jnp
from jax import lax
from jax.experimental import pallas as pl
from jax.experimental.pallas import tpu as pltpu
from jax.sharding import PartitionSpec as P

BF = jnp.bfloat16
F32 = jnp.float32
ANY = pl.BlockSpec(memory_space=pl.ANY)
LITTLE = pl.CostEstimate(flops=1, bytes_accessed=1, transcendentals=0)
ROOM = 8 * 1024 * 1024
PARTS = (2, 2, 2, 2, 2)
SPLIT = (2, 3)
CUT = 0
ORDER = (
    "down0", "sum0", "turn0", "down1:hop_b", "sum1", "residual", "hold", "see0",
    "merge0", "hop3", "down2:hop_d", "turn1", "sum2", "see1:far0", "turn2", "turn2",
    "merge1", "down3", "see2", "sum3", "turn3", "turn3", "merge2", "see3",
    "merge3", "done2", "done3", "early",
)


def _near(shape, kind):
    return pltpu.VMEM(shape, kind)


def _dot(a, b):
    return jnp.dot(a, b, preferred_element_type=F32)


def _down_kernel(half, blocks, waits, info, *refs):
    w, gives, keep = refs[blocks], refs[blocks + 1 + waits : -1], refs[-1]
    mine = info[0]
    block = refs[0][...] if blocks == 1 else jnp.where(info[1] > 0, refs[0][...], refs[1][...])
    give = _dot(block, w[:, pl.ds(pl.multiple_of((1 - mine) * half, half), half)]).astype(BF)
    count = gives[0].shape[0]
    for i, out in enumerate(gives):
        out[...] = give[i * count : (i + 1) * count]
    keep[...] = _dot(block, w[:, pl.ds(pl.multiple_of(mine * half, half), half)])


def _add_kernel(ins, outs, mine, *refs):
    came = refs[0][...] if ins == 1 else jnp.concatenate([ref[...] for ref in refs[:ins]], axis=0)
    total = (mine[...].astype(F32) + came.astype(F32)).astype(BF)
    first = 0
    for out in refs[-outs:]:
        out[...] = total[first : first + out.shape[0]]
        first += out.shape[0]


def _vision_kernel(parts, *refs):
    tokens, scale, info = refs[2 * parts], refs[2 * parts + 1], refs[2 * parts + 2]
    offset = info[0] * tokens.shape[1]
    outs, spread = refs[-3:-1], refs[-1]
    first = 0
    for mine, came in zip(refs[:parts], refs[parts : 2 * parts]):
        rows = pl.ds(first, mine.shape[0])
        for j in range(spread.shape[0]):
            lanes = pl.ds(j * 128, 128)
            scales = scale[:, pl.ds(pl.multiple_of(offset + j * 128, 128), 128)].astype(F32)
            total = mine[:, lanes].astype(F32) + came[:, lanes].astype(F32)
            vision = tokens[rows, lanes].astype(F32) + scales * total
            spread[j, rows, :] = vision.astype(BF).astype(F32)
        first += mine.shape[0]
    for j in range(spread.shape[0]):
        for k in range(4):
            out = outs[k // 2]
            out[k % 2, :, pl.ds(j * 128, 128)] = spread[j, pl.ds(k, out.shape[1], stride=4), :].astype(BF)


def _residual_kernel(half, pieces, info, tokens, *refs):
    sems, outs = refs[-1], refs[-1 - len(pieces) : -1]
    lanes = pl.ds(pl.multiple_of(info[0] * half, half), half)
    patches = tokens.shape[0] // 4
    copies = []
    for i, (block, first, count) in enumerate(pieces):
        rows = pl.ds(pl.multiple_of(info[3 + block] * patches + first, 32), count)
        copies.append(pltpu.make_async_copy(tokens.at[rows, lanes], outs[i], sems.at[i]))
        copies[-1].start()
    for copy in copies:
        copy.wait()


def _relay_kernel(first, block, *refs):
    refs[-1][...] = block[pl.ds(first, refs[-1].shape[0]), :]


def _hold_kernel(weight, *refs):
    held, sem = refs[-2:]
    copy = pltpu.make_async_copy(weight, held, sem)
    copy.start()
    copy.wait()


def _merge_kernel(half, blocks, late, first, info, *refs):
    own, other, weight = refs[: 2 * blocks], refs[2 * blocks : 4 * blocks], refs[4 * blocks]
    mine = info[0]
    here = pl.ds(pl.multiple_of(mine * half, half), half)
    there = pl.ds(pl.multiple_of((1 - mine) * half, half), half)

    def rows(these, k):
        found = [these[2 * i + k // 2][k % 2] for i in range(blocks)]
        return found[0] if blocks == 1 else jnp.concatenate(found, axis=0)

    part = None
    for k in range(4):
        more = _dot(rows(own, k), weight[k, here, :]) + _dot(rows(other, k), weight[k, there, :])
        part = more if part is None else part + more
    if late is None:
        refs[-1][...] = part.astype(BF)
        return
    near, next_to = refs[4 * blocks + 1], refs[4 * blocks + 2]
    second = info[1] > 0 if late == 0 else info[1] == 0
    found = pl.ds(first, part.shape[0])
    part = part + jnp.where(second, next_to[found, :], near[found, :]).astype(F32)
    refs[-1][...] = part
    refs[-2][...] = part.astype(BF)


def _hits(info, where_to, first, count, rows):
    index = lax.broadcasted_iota(jnp.int32, (rows, count), 0) + info[3] * rows
    return (index == where_to[:, first : first + count]).astype(F32)


def _early_kernel(parts, late, info, where_to, *refs):
    text, out, spots = refs[parts], refs[-2], refs[-1]
    projected = jnp.concatenate([ref[...] for ref in refs[:parts]], axis=0)
    rows = out.shape[0]
    to_come = _hits(info, where_to, 0, late, rows)
    hit = _hits(info, where_to, late, projected.shape[0], rows)
    image = _dot(hit.astype(BF), projected).astype(BF)
    taken = jnp.max(hit, axis=1, keepdims=True) + jnp.max(to_come, axis=1, keepdims=True)
    out[...] = jnp.where(taken > 0, image, text[...])
    spots[...] = to_come.astype(BF)


def _late_kernel(parts, base, spots, *refs):
    projected = jnp.concatenate([ref[...] for ref in refs[:parts]], axis=0)
    refs[-1][...] = (_dot(spots[...], projected) + base[...].astype(F32)).astype(BF)


def _place_kernel(parts, info, where_to, *refs):
    text, out = refs[parts], refs[-1]
    projected = jnp.concatenate([ref[...] for ref in refs[:parts]], axis=0)
    hit = _hits(info, where_to, 0, projected.shape[0], out.shape[0])
    image = _dot(hit.astype(BF), projected).astype(BF)
    out[...] = jnp.where(jnp.max(hit, axis=1, keepdims=True) > 0, image, text[...])


HBM = pl.BlockSpec(memory_space=pltpu.HBM)
VMEM = pl.BlockSpec(memory_space=pltpu.VMEM)
SMEM = pl.BlockSpec(memory_space=pltpu.SMEM)


def build(rows, cols):
    def swap(x, axis, bit):
        size = rows if axis == "row" else cols
        return lax.ppermute(x, axis, [(i, i ^ bit) for i in range(size)])

    def per_device(hidden, down_weight, tokens, layer_scale, merge_weight, text_embeds, positions):
        patches, depth = hidden.shape
        width = down_weight.shape[1]
        half = width // 2
        merged_rows = patches // 4
        dec = merge_weight.shape[2]
        row, col = lax.axis_index("row"), lax.axis_index("col")
        mine = row % 2
        inner = (col == 1) | (col == 2)
        low = col < 2
        near, far = jnp.where(low, 2, 1), jnp.where(low, 3, 0)
        info = jnp.stack([mine, inner.astype(jnp.int32), 1 - col % 2, col, col ^ 1, near, far])
        scale = layer_scale[None, :]
        row_bits = [1 << i for i in range(1, rows.bit_length() - 1)]
        after = []

        def stay(x):
            return pltpu.with_memory_space_constraint(x, pltpu.VMEM)

        def hold():
            held = pl.pallas_call(
                _hold_kernel,
                out_shape=_near(merge_weight.shape, BF),
                in_specs=[HBM] + [ANY] * len(after),
                out_specs=VMEM,
                scratch_shapes=[pltpu.SemaphoreType.DMA],
                cost_estimate=LITTLE,
                compiler_params=pltpu.CompilerParams(vmem_limit_bytes=ROOM),
                name="hold",
            )(pltpu.with_memory_space_constraint(merge_weight, pltpu.HBM), *after)
            after[:] = [held]
            return held

        def residuals(pieces):
            copies = pl.pallas_call(
                functools.partial(_residual_kernel, half, pieces),
                out_shape=tuple(_near((count, half), BF) for _, _, count in pieces),
                in_specs=[SMEM, HBM] + [ANY] * len(after),
                out_specs=(VMEM,) * len(pieces),
                scratch_shapes=[pltpu.SemaphoreType.DMA((len(pieces),))],
                cost_estimate=LITTLE,
                compiler_params=pltpu.CompilerParams(vmem_limit_bytes=ROOM),
                name="residuals",
            )(info, pltpu.with_memory_space_constraint(tokens, pltpu.HBM), *after)
            after[:] = [copies[0]]
            return copies

        def relay(block, first, count):
            same = pl.pallas_call(
                functools.partial(_relay_kernel, first),
                out_shape=_near((count, depth), BF),
                in_specs=[VMEM] + [ANY] * len(after),
                out_specs=VMEM,
                cost_estimate=LITTLE,
                compiler_params=pltpu.CompilerParams(vmem_limit_bytes=ROOM),
                name="relay",
            )(block, *after)
            after[:] = [same]
            return same

        def down(*blocks, parts=2):
            count = blocks[0].shape[0]
            *gives, keep = pl.pallas_call(
                functools.partial(_down_kernel, half, len(blocks), len(after)),
                out_shape=(_near((count // parts, half), BF),) * parts + (_near((count, half), F32),),
                in_specs=[SMEM] + [VMEM] * (len(blocks) + 1) + [ANY] * len(after),
                out_specs=(VMEM,) * (parts + 1),
                cost_estimate=LITTLE,
                compiler_params=pltpu.CompilerParams(vmem_limit_bytes=ROOM),
                name="down",
            )(info, *blocks, down_weight, *after)
            after[:] = [gives[0]]
            return tuple(gives), keep

        def add(total, came, *rows):
            counts = rows or (total.shape[0],)
            came = came if isinstance(came, tuple) else (came,)
            give = pl.pallas_call(
                functools.partial(_add_kernel, len(came), len(counts)),
                out_shape=tuple(_near((n, total.shape[1]), BF) for n in counts),
                in_specs=[VMEM] * (1 + len(came)) + [ANY] * len(after),
                out_specs=tuple(VMEM for _ in counts),
                cost_estimate=LITTLE,
                compiler_params=pltpu.CompilerParams(vmem_limit_bytes=ROOM),
                name="add",
            )(stay(total), *came, *after)
            after[:] = [give[0]]
            return give if rows else give[0]

        def see(mine_parts, came_parts, residual):
            count = residual.shape[0]
            out = pl.pallas_call(
                functools.partial(_vision_kernel, len(mine_parts)),
                out_shape=(_near((2, count // 4, half), BF),) * 2,
                in_specs=[VMEM] * (2 * len(mine_parts) + 2) + [SMEM] + [ANY] * len(after),
                out_specs=(VMEM, VMEM),
                scratch_shapes=[pltpu.VMEM((half // 128, count, 128), F32)],
                cost_estimate=LITTLE,
                compiler_params=pltpu.CompilerParams(vmem_limit_bytes=ROOM),
                name="vision",
            )(*mine_parts, *came_parts, stay(residual), scale, info, *after)
            after[:] = [out[0]]
            return tuple(out)

        def merge(own, other, weight, came=None, late=None, first=0):
            count = own[0].shape[1] * (len(own) // 2)
            extra = [] if came is None else list(came)
            outs = [_near((count, dec), BF)] + [_near((count, dec), F32)] * (len(extra) // 2)
            given = pl.pallas_call(
                functools.partial(_merge_kernel, half, len(own) // 2, late, first),
                out_shape=tuple(outs),
                in_specs=[SMEM] + [VMEM] * (2 * len(own) + 1 + len(extra)) + [ANY] * len(after),
                out_specs=(VMEM,) * len(outs),
                cost_estimate=LITTLE,
                compiler_params=pltpu.CompilerParams(vmem_limit_bytes=ROOM),
                name="merge",
            )(info, *own, *other, stay(weight), *extra, *after)
            after[:] = [given[0]]
            return given[0] if came is None else given

        def place(parts, where_to):
            return pl.pallas_call(
                functools.partial(_place_kernel, len(parts)),
                out_shape=jax.ShapeDtypeStruct(text_embeds.shape, BF),
                in_specs=[SMEM, VMEM] + [VMEM] * (len(parts) + 1) + [ANY] * len(after),
                out_specs=VMEM,
                cost_estimate=LITTLE,
                compiler_params=pltpu.CompilerParams(vmem_limit_bytes=ROOM),
                name="place",
            )(info, where_to, *parts, text_embeds, *after)

        def place_early(parts, late, where_to):
            base, spots = pl.pallas_call(
                functools.partial(_early_kernel, len(parts), late),
                out_shape=(_near(text_embeds.shape, BF), _near((text_embeds.shape[0], late), BF)),
                in_specs=[SMEM, VMEM] + [VMEM] * (len(parts) + 1) + [ANY] * len(after),
                out_specs=(VMEM, VMEM),
                cost_estimate=LITTLE,
                compiler_params=pltpu.CompilerParams(vmem_limit_bytes=ROOM),
                name="place_early",
            )(info, where_to, *parts, text_embeds, *after)
            after[:] = [spots]
            return base, spots

        def place_late(base, spots, parts):
            return pl.pallas_call(
                functools.partial(_late_kernel, len(parts)),
                out_shape=jax.ShapeDtypeStruct(text_embeds.shape, BF),
                in_specs=[VMEM] * (len(parts) + 2) + [ANY] * len(after),
                out_specs=VMEM,
                cost_estimate=LITTLE,
                compiler_params=pltpu.CompilerParams(vmem_limit_bytes=ROOM),
                name="place_late",
            )(stay(base), stay(spots), *parts, *after)

        if cols != 4:
            held = hold()
            parts = jnp.zeros((cols * merged_rows, dec), F32)
            for step in range(cols):
                block = hidden if step == 0 else swap(hidden, "col", step)
                owner = jnp.bitwise_xor(col, step)
                give, total = down(block)
                came = tuple(swap(part, "row", 1) for part in give)
                for bit in row_bits:
                    total = add(total, came)
                    came = swap(total, "row", bit)
                residual = lax.dynamic_slice(tokens, (owner * patches, mine * half), (patches, half))
                own = see([total], [came], residual)
                part = merge(own, tuple(swap(v, "row", 1) for v in own), held).astype(F32)
                parts = lax.dynamic_update_slice(parts, part, (owner * merged_rows, 0))
            return place([lax.psum(parts, "col").astype(BF)], positions[None, :])

        between, outward = [(1, 2), (2, 1)], [(1, 0), (2, 3)]
        bit_x, bit_y = (row_bits + row_bits)[:2] if row_bits else (1, 1)

        def x(give):
            return swap(give, "row", bit_x)

        def y(give):
            return swap(give, "row", bit_y)

        def core(parts):
            return tuple(swap(part, "row", 1) for part in parts)

        def pairs(give):
            return swap(give, "col", 1)

        def halves(give):
            return swap(give, "col", 2)

        at = [positions[i * merged_rows : (i + 1) * merged_rows] for i in range(4)]
        where_to = jnp.concatenate(
            [
                jnp.where(low, at[1], at[2]),
                jnp.where(low, at[0], at[3]),
                jnp.where(low, at[2], at[1]),
                jnp.where(low, at[3], at[0]),
            ]
        )[None, :]
        after.extend([scale, where_to])
        cut = CUT * patches // 7 if CUT else patches
        pieces = [(i, 0, patches) for i in range(3)] + [(3, 0, cut)]
        pieces += [(3, cut, patches - cut)] if CUT else []
        last = len(pieces)
        v = {}
        v["hop_a"] = swap(hidden, "col", 1)
        v["hop_b"] = lax.ppermute(hidden, "col", between)
        v["hop_c"] = lax.ppermute(v["hop_b"], "col", outward)
        v["hop_d"] = lax.ppermute(v["hop_a"], "col", between)

        def send_on(i):
            v["mid", i] = relay(v["hop_d"], *pieces[i][1:])
            v["hop", i] = lax.ppermute(v["mid", i], "col", outward)

        def send_down(i):
            if i < 3:
                blocks = [[hidden], [v["hop_a"]], [v["hop_b"], v["hop_c"]]][i]
            else:
                blocks = [v["mid", i], v["hop", i]]
            give, v["keep", i] = down(*blocks, parts=PARTS[i])
            v["core", i] = core(give)

        def first_sum(i):
            if i in SPLIT:
                count = pieces[i][2]
                v["sum", i] = add(v["keep", i], v["core", i], count // 2, count // 2)
                v["in", i] = [x(v["sum", i][0]), y(v["sum", i][1])]
            else:
                v["sum", i] = [add(v["keep", i], v["core", i])]
                v["in", i] = [x(v["sum", i][0])]
            v["turn", i], v["back", i] = [], []

        def second_sum(i):
            j = len(v["turn", i])
            v["turn", i].append(add(v["sum", i][j], v["in", i][j]))
            v["back", i].append((x if j else y)(v["turn", i][j]))

        def look(i):
            seen = see(v["turn", i], v["back", i], v["residual"][i])
            v["seen", i], v["other", i] = seen, core(seen)

        def project(i):
            if i < 2:
                v["far", i] = halves(merge(v["seen", i], v["other", i], v["held"]))
            else:
                block, first, _ = pieces[i]
                late = block - 2, first // 4
                give, v["part", i] = merge(v["seen", i], v["other", i], v["held"], (v["far", 0], v["far", 1]), *late)
                v["pair", i] = pairs(give)

        def complete(i):
            v["away", i] = add(v["part", i], v["pair", i])
            v["own", i] = halves(v["away", i])

        def others(name):
            if name == "hold":
                v["held"] = hold()
            elif name == "residual":
                v["residual"] = residuals(pieces)
            elif name == "early":
                v["base"] = place_early([v["away", i] for i in range(2, last)], 2 * merged_rows, where_to)

        calls = {
            "hop": send_on,
            "down": send_down,
            "sum": first_sum,
            "turn": second_sum,
            "see": look,
            "merge": project,
            "done": complete,
        }
        for step in ORDER:
            name, _, waits = step.partition(":")
            for wait in waits.split(",") if waits else ():
                after.append(v[wait if wait.startswith("hop_") else (wait[:-1], int(wait[-1]))])
            if name[:-1] in calls:
                calls[name[:-1]](int(name[-1]))
            else:
                others(name)
        return place_late(*v["base"], [v["own", i] for i in range(2, last)])

    return per_device


def solution(mesh):
    in_specs = (
        P("col", "row"),
        P("row", "col"),
        P(None, "col"),
        P("col"),
        P(None, "col", "row"),
        P("col", "row"),
        P(),
    )
    out_specs = P("col", "row")
    return jax.shard_map(
        build(mesh.shape["row"], mesh.shape["col"]),
        mesh=mesh,
        in_specs=in_specs,
        out_specs=out_specs,
        check_vma=False,
    )
```

```python
import functools

import jax
import jax.numpy as jnp
from jax import lax
from jax.experimental import pallas as pl
from jax.experimental.pallas import tpu as pltpu
from jax.sharding import PartitionSpec as P

BF = jnp.bfloat16
F32 = jnp.float32
ANY = pl.BlockSpec(memory_space=pl.ANY)
LITTLE = pl.CostEstimate(flops=1, bytes_accessed=1, transcendentals=0)
ROOM = 8 * 1024 * 1024
PARTS = (2, 2, 2, 2)
SPLIT = (2, 3)
SEEN = (2, 2, 2, 2)
ORDER = (
    "down0", "sum0", "turn0", "down1:hop_b", "sum1", "residual", "hold", "see0",
    "merge0", "hop3", "down2:hop_d", "turn1", "sum2", "see1:far0", "turn2", "turn2",
    "merge1", "down3", "see2", "sum3", "turn3:far1", "turn3:far0", "merge2", "see3:pair2",
    "merge3", "done2", "done3", "early",
)


def _near(shape, kind):
    return pltpu.VMEM(shape, kind)


def _dot(a, b):
    return jnp.dot(a, b, preferred_element_type=F32)


def _down_kernel(half, blocks, parts, info, *refs):
    w, outs = refs[blocks], refs[-parts[0] - parts[1] :]
    mine = info[0]
    block = refs[0][...] if blocks == 1 else jnp.where(info[1] > 0, refs[0][...], refs[1][...])
    if parts[0]:
        give = _dot(block, w[:, pl.ds(pl.multiple_of((1 - mine) * half, half), half)]).astype(BF)
        count = outs[0].shape[0]
        for i, out in enumerate(outs[: parts[0]]):
            out[...] = give[i * count : (i + 1) * count]
    if parts[1]:
        outs[-1][...] = _dot(block, w[:, pl.ds(pl.multiple_of(mine * half, half), half)])


def _add_kernel(ins, outs, mine, *refs):
    came = refs[0][...] if ins == 1 else jnp.concatenate([ref[...] for ref in refs[:ins]], axis=0)
    total = (mine[...].astype(F32) + came.astype(F32)).astype(BF)
    first = 0
    for out in refs[-outs:]:
        out[...] = total[first : first + out.shape[0]]
        first += out.shape[0]


def _vision_kernel(parts, seen, *refs):
    tokens, scale, info = refs[2 * parts], refs[2 * parts + 1], refs[2 * parts + 2]
    offset = info[0] * tokens.shape[1]
    outs, spread = refs[-1 - seen : -1], refs[-1]
    each = 4 // seen
    first = 0
    for mine, came in zip(refs[:parts], refs[parts : 2 * parts]):
        rows = pl.ds(first, mine.shape[0])
        for j in range(spread.shape[0]):
            lanes = pl.ds(j * 128, 128)
            scales = scale[:, pl.ds(pl.multiple_of(offset + j * 128, 128), 128)].astype(F32)
            total = mine[:, lanes].astype(F32) + came[:, lanes].astype(F32)
            vision = tokens[rows, lanes].astype(F32) + scales * total
            spread[j, rows, :] = vision.astype(BF).astype(F32)
        first += mine.shape[0]
    for j in range(spread.shape[0]):
        for k in range(4):
            out = outs[k // each]
            out[k % each, :, pl.ds(j * 128, 128)] = spread[j, pl.ds(k, out.shape[1], stride=4), :].astype(BF)


def _residual_kernel(half, pieces, info, tokens, *refs):
    sems, outs = refs[-1], refs[-1 - len(pieces) : -1]
    lanes = pl.ds(pl.multiple_of(info[0] * half, half), half)
    patches = tokens.shape[0] // 4
    copies = []
    for i, (block, first, count) in enumerate(pieces):
        rows = pl.ds(pl.multiple_of(info[3 + block] * patches + first, 32), count)
        copies.append(pltpu.make_async_copy(tokens.at[rows, lanes], outs[i], sems.at[i]))
        copies[-1].start()
    for copy in copies:
        copy.wait()


def _relay_kernel(first, block, *refs):
    refs[-1][...] = block[pl.ds(first, refs[-1].shape[0]), :]


def _hold_kernel(weight, *refs):
    held, sem = refs[-2:]
    copy = pltpu.make_async_copy(weight, held, sem)
    copy.start()
    copy.wait()


def _merge_kernel(half, blocks, late, first, info, *refs):
    own, other, weight = refs[:blocks], refs[blocks : 2 * blocks], refs[2 * blocks]
    mine = info[0]
    here = pl.ds(pl.multiple_of(mine * half, half), half)
    there = pl.ds(pl.multiple_of((1 - mine) * half, half), half)

    each = 4 // blocks
    part = None
    for k in range(4):
        i, j = k // each, k % each
        more = _dot(own[i][j], weight[k, here, :]) + _dot(other[i][j], weight[k, there, :])
        part = more if part is None else part + more
    if late is None:
        refs[-1][...] = part.astype(BF)
        return
    near, next_to = refs[2 * blocks + 1], refs[2 * blocks + 2]
    second = info[1] > 0 if late == 0 else info[1] == 0
    found = pl.ds(first, part.shape[0])
    part = part + jnp.where(second, next_to[found, :], near[found, :]).astype(F32)
    refs[-1][...] = part
    refs[-2][...] = part.astype(BF)


def _hits(info, where_to, first, count, rows):
    index = lax.broadcasted_iota(jnp.int32, (rows, count), 0) + info[3] * rows
    return (index == where_to[:, first : first + count]).astype(F32)


def _early_kernel(parts, late, info, where_to, *refs):
    text, out, spots = refs[parts], refs[-2], refs[-1]
    projected = jnp.concatenate([ref[...] for ref in refs[:parts]], axis=0)
    rows = out.shape[0]
    to_come = _hits(info, where_to, 0, late, rows)
    hit = _hits(info, where_to, late, projected.shape[0], rows)
    image = _dot(hit.astype(BF), projected).astype(BF)
    taken = jnp.max(hit, axis=1, keepdims=True) + jnp.max(to_come, axis=1, keepdims=True)
    out[...] = jnp.where(taken > 0, image, text[...])
    spots[...] = to_come.astype(BF)


def _late_kernel(parts, base, spots, *refs):
    projected = jnp.concatenate([ref[...] for ref in refs[:parts]], axis=0)
    refs[-1][...] = (_dot(spots[...], projected) + base[...].astype(F32)).astype(BF)


def _place_kernel(parts, info, where_to, *refs):
    text, out = refs[parts], refs[-1]
    projected = jnp.concatenate([ref[...] for ref in refs[:parts]], axis=0)
    hit = _hits(info, where_to, 0, projected.shape[0], out.shape[0])
    image = _dot(hit.astype(BF), projected).astype(BF)
    out[...] = jnp.where(jnp.max(hit, axis=1, keepdims=True) > 0, image, text[...])


HBM = pl.BlockSpec(memory_space=pltpu.HBM)
VMEM = pl.BlockSpec(memory_space=pltpu.VMEM)
SMEM = pl.BlockSpec(memory_space=pltpu.SMEM)


def build(rows, cols):
    def swap(x, axis, bit):
        size = rows if axis == "row" else cols
        return lax.ppermute(x, axis, [(i, i ^ bit) for i in range(size)])

    def per_device(hidden, down_weight, tokens, layer_scale, merge_weight, text_embeds, positions):
        patches, depth = hidden.shape
        width = down_weight.shape[1]
        half = width // 2
        merged_rows = patches // 4
        dec = merge_weight.shape[2]
        row, col = lax.axis_index("row"), lax.axis_index("col")
        mine = row % 2
        inner = (col == 1) | (col == 2)
        low = col < 2
        near, far = jnp.where(low, 2, 1), jnp.where(low, 3, 0)
        info = jnp.stack([mine, inner.astype(jnp.int32), 1 - col % 2, col, col ^ 1, near, far])
        scale = layer_scale[None, :]
        row_bits = [1 << i for i in range(1, rows.bit_length() - 1)]
        after = []

        def stay(x):
            return pltpu.with_memory_space_constraint(x, pltpu.VMEM)

        def hold():
            held = pl.pallas_call(
                _hold_kernel,
                out_shape=_near(merge_weight.shape, BF),
                in_specs=[HBM] + [ANY] * len(after),
                out_specs=VMEM,
                scratch_shapes=[pltpu.SemaphoreType.DMA],
                cost_estimate=LITTLE,
                compiler_params=pltpu.CompilerParams(vmem_limit_bytes=ROOM),
                name="hold",
            )(pltpu.with_memory_space_constraint(merge_weight, pltpu.HBM), *after)
            after[:] = [held]
            return held

        def residuals(pieces):
            copies = pl.pallas_call(
                functools.partial(_residual_kernel, half, pieces),
                out_shape=tuple(_near((count, half), BF) for _, _, count in pieces),
                in_specs=[SMEM, HBM] + [ANY] * len(after),
                out_specs=(VMEM,) * len(pieces),
                scratch_shapes=[pltpu.SemaphoreType.DMA((len(pieces),))],
                cost_estimate=LITTLE,
                compiler_params=pltpu.CompilerParams(vmem_limit_bytes=ROOM),
                name="residuals",
            )(info, pltpu.with_memory_space_constraint(tokens, pltpu.HBM), *after)
            after[:] = [copies[0]]
            return copies

        def relay(block, first, count):
            same = pl.pallas_call(
                functools.partial(_relay_kernel, first),
                out_shape=_near((count, depth), BF),
                in_specs=[VMEM] + [ANY] * len(after),
                out_specs=VMEM,
                cost_estimate=LITTLE,
                compiler_params=pltpu.CompilerParams(vmem_limit_bytes=ROOM),
                name="relay",
            )(block, *after)
            after[:] = [same]
            return same

        def down(*blocks, parts=2, keep=1):
            count = blocks[0].shape[0]
            outs = [_near((count // parts, half), BF)] * parts if parts else []
            outs += [_near((count, half), F32)] * keep
            given = pl.pallas_call(
                functools.partial(_down_kernel, half, len(blocks), (parts, keep)),
                out_shape=tuple(outs),
                in_specs=[SMEM] + [VMEM] * (len(blocks) + 1) + [ANY] * len(after),
                out_specs=(VMEM,) * len(outs),
                cost_estimate=LITTLE,
                compiler_params=pltpu.CompilerParams(vmem_limit_bytes=ROOM),
                name="down",
            )(info, *blocks, down_weight, *after)
            after[:] = [given[0]]
            return tuple(given[:parts]), given[-1]

        def add(total, came, *rows):
            counts = rows or (total.shape[0],)
            came = came if isinstance(came, tuple) else (came,)
            give = pl.pallas_call(
                functools.partial(_add_kernel, len(came), len(counts)),
                out_shape=tuple(_near((n, total.shape[1]), BF) for n in counts),
                in_specs=[VMEM] * (1 + len(came)) + [ANY] * len(after),
                out_specs=tuple(VMEM for _ in counts),
                cost_estimate=LITTLE,
                compiler_params=pltpu.CompilerParams(vmem_limit_bytes=ROOM),
                name="add",
            )(stay(total), *came, *after)
            after[:] = [give[0]]
            return give if rows else give[0]

        def see(mine_parts, came_parts, residual, parts=2):
            count = residual.shape[0]
            out = pl.pallas_call(
                functools.partial(_vision_kernel, len(mine_parts), parts),
                out_shape=(_near((4 // parts, count // 4, half), BF),) * parts,
                in_specs=[VMEM] * (2 * len(mine_parts) + 2) + [SMEM] + [ANY] * len(after),
                out_specs=(VMEM,) * parts,
                scratch_shapes=[pltpu.VMEM((half // 128, count, 128), F32)],
                cost_estimate=LITTLE,
                compiler_params=pltpu.CompilerParams(vmem_limit_bytes=ROOM),
                name="vision",
            )(*mine_parts, *came_parts, stay(residual), scale, info, *after)
            after[:] = [out[0]]
            return tuple(out)

        def merge(own, other, weight, came=None, late=None, first=0):
            count = own[0].shape[1]
            extra = [] if came is None else list(came)
            outs = [_near((count, dec), BF)] + [_near((count, dec), F32)] * (len(extra) // 2)
            given = pl.pallas_call(
                functools.partial(_merge_kernel, half, len(own), late, first),
                out_shape=tuple(outs),
                in_specs=[SMEM] + [VMEM] * (2 * len(own) + 1 + len(extra)) + [ANY] * len(after),
                out_specs=(VMEM,) * len(outs),
                cost_estimate=LITTLE,
                compiler_params=pltpu.CompilerParams(vmem_limit_bytes=ROOM),
                name="merge",
            )(info, *own, *other, stay(weight), *extra, *after)
            after[:] = [given[0]]
            return given[0] if came is None else given

        def place(parts, where_to):
            return pl.pallas_call(
                functools.partial(_place_kernel, len(parts)),
                out_shape=jax.ShapeDtypeStruct(text_embeds.shape, BF),
                in_specs=[SMEM, VMEM] + [VMEM] * (len(parts) + 1) + [ANY] * len(after),
                out_specs=VMEM,
                cost_estimate=LITTLE,
                compiler_params=pltpu.CompilerParams(vmem_limit_bytes=ROOM),
                name="place",
            )(info, where_to, *parts, text_embeds, *after)

        def place_early(parts, late, where_to):
            base, spots = pl.pallas_call(
                functools.partial(_early_kernel, len(parts), late),
                out_shape=(_near(text_embeds.shape, BF), _near((text_embeds.shape[0], late), BF)),
                in_specs=[SMEM, VMEM] + [VMEM] * (len(parts) + 1) + [ANY] * len(after),
                out_specs=(VMEM, VMEM),
                cost_estimate=LITTLE,
                compiler_params=pltpu.CompilerParams(vmem_limit_bytes=ROOM),
                name="place_early",
            )(info, where_to, *parts, text_embeds, *after)
            after[:] = [spots]
            return base, spots

        def place_late(base, spots, parts):
            return pl.pallas_call(
                functools.partial(_late_kernel, len(parts)),
                out_shape=jax.ShapeDtypeStruct(text_embeds.shape, BF),
                in_specs=[VMEM] * (len(parts) + 2) + [ANY] * len(after),
                out_specs=VMEM,
                cost_estimate=LITTLE,
                compiler_params=pltpu.CompilerParams(vmem_limit_bytes=ROOM),
                name="place_late",
            )(stay(base), stay(spots), *parts, *after)

        if cols != 4:
            held = hold()
            parts = jnp.zeros((cols * merged_rows, dec), F32)
            for step in range(cols):
                block = hidden if step == 0 else swap(hidden, "col", step)
                owner = jnp.bitwise_xor(col, step)
                give, total = down(block)
                came = tuple(swap(part, "row", 1) for part in give)
                for bit in row_bits:
                    total = add(total, came)
                    came = swap(total, "row", bit)
                residual = lax.dynamic_slice(tokens, (owner * patches, mine * half), (patches, half))
                own = see([total], [came], residual)
                part = merge(own, tuple(swap(v, "row", 1) for v in own), held).astype(F32)
                parts = lax.dynamic_update_slice(parts, part, (owner * merged_rows, 0))
            return place([lax.psum(parts, "col").astype(BF)], positions[None, :])

        between, outward = [(1, 2), (2, 1)], [(1, 0), (2, 3)]
        bit_x, bit_y = (row_bits + row_bits)[:2] if row_bits else (1, 1)

        def x(give):
            return swap(give, "row", bit_x)

        def y(give):
            return swap(give, "row", bit_y)

        def core(parts):
            return tuple(swap(part, "row", 1) for part in parts)

        def pairs(give):
            return swap(give, "col", 1)

        def halves(give):
            return swap(give, "col", 2)

        at = [positions[i * merged_rows : (i + 1) * merged_rows] for i in range(4)]
        where_to = jnp.concatenate(
            [
                jnp.where(low, at[1], at[2]),
                jnp.where(low, at[0], at[3]),
                jnp.where(low, at[2], at[1]),
                jnp.where(low, at[3], at[0]),
            ]
        )[None, :]
        after.extend([scale, where_to])
        pieces = [(i, 0, patches) for i in range(4)]
        last = len(pieces)
        v = {}
        v["hop_a"] = swap(hidden, "col", 1)
        v["hop_b"] = lax.ppermute(hidden, "col", between)
        v["hop_c"] = lax.ppermute(v["hop_b"], "col", outward)
        v["hop_d"] = lax.ppermute(v["hop_a"], "col", between)

        def send_on(i):
            v["mid", i] = relay(v["hop_d"], *pieces[i][1:])
            v["hop", i] = lax.ppermute(v["mid", i], "col", outward)

        def send_down(i):
            if i < 3:
                blocks = [[hidden], [v["hop_a"]], [v["hop_b"], v["hop_c"]]][i]
            else:
                blocks = [v["mid", i], v["hop", i]]
            v["block", i] = blocks
            give, v["keep", i] = down(*blocks, parts=PARTS[i], keep=0 if f"keep{i}" in ORDER else 1)
            v["core", i] = core(give)

        def stay_down(i):
            _, v["keep", i] = down(*v["block", i], parts=0)

        def first_sum(i):
            if i in SPLIT:
                count = pieces[i][2]
                v["sum", i] = add(v["keep", i], v["core", i], count // 2, count // 2)
                v["in", i] = [x(v["sum", i][0]), y(v["sum", i][1])]
            else:
                v["sum", i] = [add(v["keep", i], v["core", i])]
                v["in", i] = [x(v["sum", i][0])]
            v["turn", i], v["back", i] = [], []

        def second_sum(i):
            j = len(v["turn", i])
            v["turn", i].append(add(v["sum", i][j], v["in", i][j]))
            v["back", i].append((x if j else y)(v["turn", i][j]))

        def look(i):
            seen = see(v["turn", i], v["back", i], v["residual"][i], SEEN[i])
            v["seen", i], v["other", i] = seen, core(seen)

        def project(i):
            if i < 2:
                v["far", i] = halves(merge(v["seen", i], v["other", i], v["held"]))
            else:
                block, first, _ = pieces[i]
                late = block - 2, first // 4
                give, v["part", i] = merge(v["seen", i], v["other", i], v["held"], (v["far", 0], v["far", 1]), *late)
                v["pair", i] = pairs(give)

        def complete(i):
            v["away", i] = add(v["part", i], v["pair", i])
            v["own", i] = halves(v["away", i])

        def others(name):
            if name == "hold":
                v["held"] = hold()
            elif name == "residual":
                v["residual"] = residuals(pieces)
            elif name == "early":
                v["base"] = place_early([v["away", i] for i in range(2, last)], 2 * merged_rows, where_to)

        calls = {
            "hop": send_on,
            "down": send_down,
            "keep": stay_down,
            "sum": first_sum,
            "turn": second_sum,
            "see": look,
            "merge": project,
            "done": complete,
        }
        for step in ORDER:
            name, _, waits = step.partition(":")
            for wait in waits.split(",") if waits else ():
                after.append(v[wait if wait.startswith("hop_") else (wait[:-1], int(wait[-1]))])
            if name[:-1] in calls:
                calls[name[:-1]](int(name[-1]))
            else:
                others(name)
        return place_late(*v["base"], [v["own", i] for i in range(2, last)])

    return per_device


def solution(mesh):
    in_specs = (
        P("col", "row"),
        P("row", "col"),
        P(None, "col"),
        P("col"),
        P(None, "col", "row"),
        P("col", "row"),
        P(),
    )
    out_specs = P("col", "row")
    return jax.shard_map(
        build(mesh.shape["row"], mesh.shape["col"]),
        mesh=mesh,
        in_specs=in_specs,
        out_specs=out_specs,
        check_vma=False,
    )
```

```python
import functools

import jax
import jax.numpy as jnp
from jax import lax
from jax.experimental import pallas as pl
from jax.experimental.pallas import tpu as pltpu
from jax.sharding import PartitionSpec as P

BF = jnp.bfloat16
F32 = jnp.float32
ANY = pl.BlockSpec(memory_space=pl.ANY)
LITTLE = pl.CostEstimate(flops=1, bytes_accessed=1, transcendentals=0)
ROOM = 8 * 1024 * 1024
PARTS = (2, 2, 2, 2)
SPLIT = (2, 3)
SEEN = (2, 2, 2, 2)
ORDER = (
    "down0", "sum0", "turn0", "down1:hop_b", "sum1", "residual", "hold", "see0",
    "merge0", "hop3", "down2:hop_d", "turn1", "sum2", "see1:far0", "turn2", "turn2",
    "merge1", "down3", "see2", "sum3", "turn3:far1", "turn3:far0", "merge2", "see3:pair2",
    "head3", "merge3", "done2", "done3", "early",
)


def _near(shape, kind):
    return pltpu.VMEM(shape, kind)


def _dot(a, b):
    return jnp.dot(a, b, preferred_element_type=F32)


def _down_kernel(half, blocks, parts, info, *refs):
    w, outs = refs[blocks], refs[-parts[0] - parts[1] :]
    mine = info[0]
    block = refs[0][...] if blocks == 1 else jnp.where(info[1] > 0, refs[0][...], refs[1][...])
    if parts[0]:
        give = _dot(block, w[:, pl.ds(pl.multiple_of((1 - mine) * half, half), half)]).astype(BF)
        count = outs[0].shape[0]
        for i, out in enumerate(outs[: parts[0]]):
            out[...] = give[i * count : (i + 1) * count]
    if parts[1]:
        outs[-1][...] = _dot(block, w[:, pl.ds(pl.multiple_of(mine * half, half), half)])


def _add_kernel(ins, outs, mine, *refs):
    came = refs[0][...] if ins == 1 else jnp.concatenate([ref[...] for ref in refs[:ins]], axis=0)
    total = (mine[...].astype(F32) + came.astype(F32)).astype(BF)
    first = 0
    for out in refs[-outs:]:
        out[...] = total[first : first + out.shape[0]]
        first += out.shape[0]


def _vision_kernel(parts, seen, *refs):
    tokens, scale, info = refs[2 * parts], refs[2 * parts + 1], refs[2 * parts + 2]
    offset = info[0] * tokens.shape[1]
    outs, spread = refs[-1 - seen : -1], refs[-1]
    each = 4 // seen
    first = 0
    for mine, came in zip(refs[:parts], refs[parts : 2 * parts]):
        rows = pl.ds(first, mine.shape[0])
        for j in range(spread.shape[0]):
            lanes = pl.ds(j * 128, 128)
            scales = scale[:, pl.ds(pl.multiple_of(offset + j * 128, 128), 128)].astype(F32)
            total = mine[:, lanes].astype(F32) + came[:, lanes].astype(F32)
            vision = tokens[rows, lanes].astype(F32) + scales * total
            spread[j, rows, :] = vision.astype(BF).astype(F32)
        first += mine.shape[0]
    for j in range(spread.shape[0]):
        for k in range(4):
            out = outs[k // each]
            out[k % each, :, pl.ds(j * 128, 128)] = spread[j, pl.ds(k, out.shape[1], stride=4), :].astype(BF)


def _residual_kernel(half, pieces, info, tokens, *refs):
    sems, outs = refs[-1], refs[-1 - len(pieces) : -1]
    lanes = pl.ds(pl.multiple_of(info[0] * half, half), half)
    patches = tokens.shape[0] // 4
    copies = []
    for i, (block, first, count) in enumerate(pieces):
        rows = pl.ds(pl.multiple_of(info[3 + block] * patches + first, 32), count)
        copies.append(pltpu.make_async_copy(tokens.at[rows, lanes], outs[i], sems.at[i]))
        copies[-1].start()
    for copy in copies:
        copy.wait()


def _relay_kernel(first, block, *refs):
    refs[-1][...] = block[pl.ds(first, refs[-1].shape[0]), :]


def _hold_kernel(weight, *refs):
    held, sem = refs[-2:]
    copy = pltpu.make_async_copy(weight, held, sem)
    copy.start()
    copy.wait()


def _head_kernel(half, blocks, info, *refs):
    own, weight = refs[:blocks], refs[blocks]
    here = pl.ds(pl.multiple_of(info[0] * half, half), half)
    each = 4 // blocks
    part = None
    for k in range(4):
        more = _dot(own[k // each][k % each], weight[k, here, :])
        part = more if part is None else part + more
    refs[-1][...] = part


def _merge_kernel(half, blocks, late, first, head, info, *refs):
    own, other, weight = refs[:blocks], refs[blocks : 2 * blocks], refs[2 * blocks]
    mine = info[0]
    here = pl.ds(pl.multiple_of(mine * half, half), half)
    there = pl.ds(pl.multiple_of((1 - mine) * half, half), half)

    each = 4 // blocks
    part = refs[2 * blocks + 3][...] if head else None
    for k in range(4):
        i, j = k // each, k % each
        more = _dot(other[i][j], weight[k, there, :])
        if not head:
            more = more + _dot(own[i][j], weight[k, here, :])
        part = more if part is None else part + more
    if late is None:
        refs[-1][...] = part.astype(BF)
        return
    near, next_to = refs[2 * blocks + 1], refs[2 * blocks + 2]
    second = info[1] > 0 if late == 0 else info[1] == 0
    found = pl.ds(first, part.shape[0])
    part = part + jnp.where(second, next_to[found, :], near[found, :]).astype(F32)
    refs[-1][...] = part
    refs[-2][...] = part.astype(BF)


def _hits(info, where_to, first, count, rows):
    index = lax.broadcasted_iota(jnp.int32, (rows, count), 0) + info[3] * rows
    return (index == where_to[:, first : first + count]).astype(F32)


def _early_kernel(parts, late, info, where_to, *refs):
    text, out, spots = refs[parts], refs[-2], refs[-1]
    projected = jnp.concatenate([ref[...] for ref in refs[:parts]], axis=0)
    rows = out.shape[0]
    to_come = _hits(info, where_to, 0, late, rows)
    hit = _hits(info, where_to, late, projected.shape[0], rows)
    image = _dot(hit.astype(BF), projected).astype(BF)
    taken = jnp.max(hit, axis=1, keepdims=True) + jnp.max(to_come, axis=1, keepdims=True)
    out[...] = jnp.where(taken > 0, image, text[...])
    spots[...] = to_come.astype(BF)


def _late_kernel(parts, base, spots, *refs):
    projected = jnp.concatenate([ref[...] for ref in refs[:parts]], axis=0)
    refs[-1][...] = (_dot(spots[...], projected) + base[...].astype(F32)).astype(BF)


def _place_kernel(parts, info, where_to, *refs):
    text, out = refs[parts], refs[-1]
    projected = jnp.concatenate([ref[...] for ref in refs[:parts]], axis=0)
    hit = _hits(info, where_to, 0, projected.shape[0], out.shape[0])
    image = _dot(hit.astype(BF), projected).astype(BF)
    out[...] = jnp.where(jnp.max(hit, axis=1, keepdims=True) > 0, image, text[...])


HBM = pl.BlockSpec(memory_space=pltpu.HBM)
VMEM = pl.BlockSpec(memory_space=pltpu.VMEM)
SMEM = pl.BlockSpec(memory_space=pltpu.SMEM)


def build(rows, cols):
    def swap(x, axis, bit):
        size = rows if axis == "row" else cols
        return lax.ppermute(x, axis, [(i, i ^ bit) for i in range(size)])

    def per_device(hidden, down_weight, tokens, layer_scale, merge_weight, text_embeds, positions):
        patches, depth = hidden.shape
        width = down_weight.shape[1]
        half = width // 2
        merged_rows = patches // 4
        dec = merge_weight.shape[2]
        row, col = lax.axis_index("row"), lax.axis_index("col")
        mine = row % 2
        inner = (col == 1) | (col == 2)
        low = col < 2
        near, far = jnp.where(low, 2, 1), jnp.where(low, 3, 0)
        info = jnp.stack([mine, inner.astype(jnp.int32), 1 - col % 2, col, col ^ 1, near, far])
        scale = layer_scale[None, :]
        row_bits = [1 << i for i in range(1, rows.bit_length() - 1)]
        after = []

        def stay(x):
            return pltpu.with_memory_space_constraint(x, pltpu.VMEM)

        def hold():
            held = pl.pallas_call(
                _hold_kernel,
                out_shape=_near(merge_weight.shape, BF),
                in_specs=[HBM] + [ANY] * len(after),
                out_specs=VMEM,
                scratch_shapes=[pltpu.SemaphoreType.DMA],
                cost_estimate=LITTLE,
                compiler_params=pltpu.CompilerParams(vmem_limit_bytes=ROOM),
                name="hold",
            )(pltpu.with_memory_space_constraint(merge_weight, pltpu.HBM), *after)
            after[:] = [held]
            return held

        def residuals(pieces):
            copies = pl.pallas_call(
                functools.partial(_residual_kernel, half, pieces),
                out_shape=tuple(_near((count, half), BF) for _, _, count in pieces),
                in_specs=[SMEM, HBM] + [ANY] * len(after),
                out_specs=(VMEM,) * len(pieces),
                scratch_shapes=[pltpu.SemaphoreType.DMA((len(pieces),))],
                cost_estimate=LITTLE,
                compiler_params=pltpu.CompilerParams(vmem_limit_bytes=ROOM),
                name="residuals",
            )(info, pltpu.with_memory_space_constraint(tokens, pltpu.HBM), *after)
            after[:] = [copies[0]]
            return copies

        def relay(block, first, count):
            same = pl.pallas_call(
                functools.partial(_relay_kernel, first),
                out_shape=_near((count, depth), BF),
                in_specs=[VMEM] + [ANY] * len(after),
                out_specs=VMEM,
                cost_estimate=LITTLE,
                compiler_params=pltpu.CompilerParams(vmem_limit_bytes=ROOM),
                name="relay",
            )(block, *after)
            after[:] = [same]
            return same

        def down(*blocks, parts=2, keep=1):
            count = blocks[0].shape[0]
            outs = [_near((count // parts, half), BF)] * parts if parts else []
            outs += [_near((count, half), F32)] * keep
            given = pl.pallas_call(
                functools.partial(_down_kernel, half, len(blocks), (parts, keep)),
                out_shape=tuple(outs),
                in_specs=[SMEM] + [VMEM] * (len(blocks) + 1) + [ANY] * len(after),
                out_specs=(VMEM,) * len(outs),
                cost_estimate=LITTLE,
                compiler_params=pltpu.CompilerParams(vmem_limit_bytes=ROOM),
                name="down",
            )(info, *blocks, down_weight, *after)
            after[:] = [given[0]]
            return tuple(given[:parts]), given[-1]

        def add(total, came, *rows):
            counts = rows or (total.shape[0],)
            came = came if isinstance(came, tuple) else (came,)
            give = pl.pallas_call(
                functools.partial(_add_kernel, len(came), len(counts)),
                out_shape=tuple(_near((n, total.shape[1]), BF) for n in counts),
                in_specs=[VMEM] * (1 + len(came)) + [ANY] * len(after),
                out_specs=tuple(VMEM for _ in counts),
                cost_estimate=LITTLE,
                compiler_params=pltpu.CompilerParams(vmem_limit_bytes=ROOM),
                name="add",
            )(stay(total), *came, *after)
            after[:] = [give[0]]
            return give if rows else give[0]

        def see(mine_parts, came_parts, residual, parts=2):
            count = residual.shape[0]
            out = pl.pallas_call(
                functools.partial(_vision_kernel, len(mine_parts), parts),
                out_shape=(_near((4 // parts, count // 4, half), BF),) * parts,
                in_specs=[VMEM] * (2 * len(mine_parts) + 2) + [SMEM] + [ANY] * len(after),
                out_specs=(VMEM,) * parts,
                scratch_shapes=[pltpu.VMEM((half // 128, count, 128), F32)],
                cost_estimate=LITTLE,
                compiler_params=pltpu.CompilerParams(vmem_limit_bytes=ROOM),
                name="vision",
            )(*mine_parts, *came_parts, stay(residual), scale, info, *after)
            after[:] = [out[0]]
            return tuple(out)

        def merge_head(own, weight):
            count = own[0].shape[1]
            part = pl.pallas_call(
                functools.partial(_head_kernel, half, len(own)),
                out_shape=_near((count, dec), F32),
                in_specs=[SMEM] + [VMEM] * (len(own) + 1) + [ANY] * len(after),
                out_specs=VMEM,
                cost_estimate=LITTLE,
                compiler_params=pltpu.CompilerParams(vmem_limit_bytes=ROOM),
                name="merge_head",
            )(info, *own, stay(weight), *after)
            after[:] = [part]
            return part

        def merge(own, other, weight, came=None, late=None, first=0, head=None):
            count = own[0].shape[1]
            extra = [] if came is None else list(came)
            extra += [] if head is None else [stay(head)]
            outs = [_near((count, dec), BF)] + [_near((count, dec), F32)] * (came is not None)
            given = pl.pallas_call(
                functools.partial(_merge_kernel, half, len(own), late, first, head is not None),
                out_shape=tuple(outs),
                in_specs=[SMEM] + [VMEM] * (2 * len(own) + 1 + len(extra)) + [ANY] * len(after),
                out_specs=(VMEM,) * len(outs),
                cost_estimate=LITTLE,
                compiler_params=pltpu.CompilerParams(vmem_limit_bytes=ROOM),
                name="merge",
            )(info, *own, *other, stay(weight), *extra, *after)
            after[:] = [given[0]]
            return given[0] if came is None else given

        def place(parts, where_to):
            return pl.pallas_call(
                functools.partial(_place_kernel, len(parts)),
                out_shape=jax.ShapeDtypeStruct(text_embeds.shape, BF),
                in_specs=[SMEM, VMEM] + [VMEM] * (len(parts) + 1) + [ANY] * len(after),
                out_specs=VMEM,
                cost_estimate=LITTLE,
                compiler_params=pltpu.CompilerParams(vmem_limit_bytes=ROOM),
                name="place",
            )(info, where_to, *parts, text_embeds, *after)

        def place_early(parts, late, where_to):
            base, spots = pl.pallas_call(
                functools.partial(_early_kernel, len(parts), late),
                out_shape=(_near(text_embeds.shape, BF), _near((text_embeds.shape[0], late), BF)),
                in_specs=[SMEM, VMEM] + [VMEM] * (len(parts) + 1) + [ANY] * len(after),
                out_specs=(VMEM, VMEM),
                cost_estimate=LITTLE,
                compiler_params=pltpu.CompilerParams(vmem_limit_bytes=ROOM),
                name="place_early",
            )(info, where_to, *parts, text_embeds, *after)
            after[:] = [spots]
            return base, spots

        def place_late(base, spots, parts):
            return pl.pallas_call(
                functools.partial(_late_kernel, len(parts)),
                out_shape=jax.ShapeDtypeStruct(text_embeds.shape, BF),
                in_specs=[VMEM] * (len(parts) + 2) + [ANY] * len(after),
                out_specs=VMEM,
                cost_estimate=LITTLE,
                compiler_params=pltpu.CompilerParams(vmem_limit_bytes=ROOM),
                name="place_late",
            )(stay(base), stay(spots), *parts, *after)

        if cols != 4:
            held = hold()
            parts = jnp.zeros((cols * merged_rows, dec), F32)
            for step in range(cols):
                block = hidden if step == 0 else swap(hidden, "col", step)
                owner = jnp.bitwise_xor(col, step)
                give, total = down(block)
                came = tuple(swap(part, "row", 1) for part in give)
                for bit in row_bits:
                    total = add(total, came)
                    came = swap(total, "row", bit)
                residual = lax.dynamic_slice(tokens, (owner * patches, mine * half), (patches, half))
                own = see([total], [came], residual)
                part = merge(own, tuple(swap(v, "row", 1) for v in own), held).astype(F32)
                parts = lax.dynamic_update_slice(parts, part, (owner * merged_rows, 0))
            return place([lax.psum(parts, "col").astype(BF)], positions[None, :])

        between, outward = [(1, 2), (2, 1)], [(1, 0), (2, 3)]
        bit_x, bit_y = (row_bits + row_bits)[:2] if row_bits else (1, 1)

        def x(give):
            return swap(give, "row", bit_x)

        def y(give):
            return swap(give, "row", bit_y)

        def core(parts):
            return tuple(swap(part, "row", 1) for part in parts)

        def pairs(give):
            return swap(give, "col", 1)

        def halves(give):
            return swap(give, "col", 2)

        at = [positions[i * merged_rows : (i + 1) * merged_rows] for i in range(4)]
        where_to = jnp.concatenate(
            [
                jnp.where(low, at[1], at[2]),
                jnp.where(low, at[0], at[3]),
                jnp.where(low, at[2], at[1]),
                jnp.where(low, at[3], at[0]),
            ]
        )[None, :]
        after.extend([scale, where_to])
        pieces = [(i, 0, patches) for i in range(4)]
        last = len(pieces)
        v = {}
        v["hop_a"] = swap(hidden, "col", 1)
        v["hop_b"] = lax.ppermute(hidden, "col", between)
        v["hop_c"] = lax.ppermute(v["hop_b"], "col", outward)
        v["hop_d"] = lax.ppermute(v["hop_a"], "col", between)

        def send_on(i):
            v["mid", i] = relay(v["hop_d"], *pieces[i][1:])
            v["hop", i] = lax.ppermute(v["mid", i], "col", outward)

        def send_down(i):
            if i < 3:
                blocks = [[hidden], [v["hop_a"]], [v["hop_b"], v["hop_c"]]][i]
            else:
                blocks = [v["mid", i], v["hop", i]]
            v["block", i] = blocks
            give, v["keep", i] = down(*blocks, parts=PARTS[i], keep=0 if f"keep{i}" in ORDER else 1)
            v["core", i] = core(give)

        def stay_down(i):
            _, v["keep", i] = down(*v["block", i], parts=0)

        def first_sum(i):
            if i in SPLIT:
                count = pieces[i][2]
                v["sum", i] = add(v["keep", i], v["core", i], count // 2, count // 2)
                v["in", i] = [x(v["sum", i][0]), y(v["sum", i][1])]
            else:
                v["sum", i] = [add(v["keep", i], v["core", i])]
                v["in", i] = [x(v["sum", i][0])]
            v["turn", i], v["back", i] = [], []

        def second_sum(i):
            j = len(v["turn", i])
            v["turn", i].append(add(v["sum", i][j], v["in", i][j]))
            v["back", i].append((x if j else y)(v["turn", i][j]))

        def look(i):
            seen = see(v["turn", i], v["back", i], v["residual"][i], SEEN[i])
            v["seen", i], v["other", i] = seen, core(seen)

        def project(i):
            if i < 2:
                v["far", i] = halves(merge(v["seen", i], v["other", i], v["held"]))
            else:
                block, first, _ = pieces[i]
                late = block - 2, first // 4
                give, v["part", i] = merge(v["seen", i], v["other", i], v["held"], (v["far", 0], v["far", 1]), *late, v.get(("head", i)))
                v["pair", i] = pairs(give)

        def project_head(i):
            v["head", i] = merge_head(v["seen", i], v["held"])

        def complete(i):
            v["away", i] = add(v["part", i], v["pair", i])
            v["own", i] = halves(v["away", i])

        def others(name):
            if name == "hold":
                v["held"] = hold()
            elif name == "residual":
                v["residual"] = residuals(pieces)
            elif name == "early":
                v["base"] = place_early([v["away", i] for i in range(2, last)], 2 * merged_rows, where_to)

        calls = {
            "hop": send_on,
            "down": send_down,
            "keep": stay_down,
            "sum": first_sum,
            "turn": second_sum,
            "see": look,
            "merge": project,
            "head": project_head,
            "done": complete,
        }
        for step in ORDER:
            name, _, waits = step.partition(":")
            for wait in waits.split(",") if waits else ():
                after.append(v[wait if wait.startswith("hop_") else (wait[:-1], int(wait[-1]))])
            if name[:-1] in calls:
                calls[name[:-1]](int(name[-1]))
            else:
                others(name)
        return place_late(*v["base"], [v["own", i] for i in range(2, last)])

    return per_device


def solution(mesh):
    in_specs = (
        P("col", "row"),
        P("row", "col"),
        P(None, "col"),
        P("col"),
        P(None, "col", "row"),
        P("col", "row"),
        P(),
    )
    out_specs = P("col", "row")
    return jax.shard_map(
        build(mesh.shape["row"], mesh.shape["col"]),
        mesh=mesh,
        in_specs=in_specs,
        out_specs=out_specs,
        check_vma=False,
    )
```

```python
import functools

import jax
import jax.numpy as jnp
from jax import lax
from jax.experimental import pallas as pl
from jax.experimental.pallas import tpu as pltpu
from jax.sharding import PartitionSpec as P

BF = jnp.bfloat16
F32 = jnp.float32
ANY = pl.BlockSpec(memory_space=pl.ANY)
LITTLE = pl.CostEstimate(flops=1, bytes_accessed=1, transcendentals=0)
ROOM = 8 * 1024 * 1024
PARTS = (2, 2, 2, 2)
SPLIT = (2, 3)
SEEN = (2, 2, 2, 2)
ORDER = (
    "down0", "sum0", "turn0", "down1:hop_b", "sum1", "residual", "hold", "see0",
    "merge0", "hop3", "down2:hop_d", "turn1", "sum2", "see1:far0", "turn2", "turn2",
    "merge1", "down3", "see2", "sum3", "turn3:far1", "turn3:far0", "merge2", "see3:pair2",
    "head3", "merge3", "done2", "done3", "early",
)


def _near(shape, kind):
    return pltpu.VMEM(shape, kind)


def _dot(a, b):
    return jnp.dot(a, b, preferred_element_type=F32)


def _down_kernel(half, blocks, parts, info, *refs):
    w, outs = refs[blocks], refs[-parts[0] - parts[1] :]
    mine = info[0]
    block = refs[0][...] if blocks == 1 else jnp.where(info[1] > 0, refs[0][...], refs[1][...])
    if parts[0]:
        give = _dot(block, w[:, pl.ds(pl.multiple_of((1 - mine) * half, half), half)]).astype(BF)
        count = outs[0].shape[0]
        for i, out in enumerate(outs[: parts[0]]):
            out[...] = give[i * count : (i + 1) * count]
    if parts[1]:
        outs[-1][...] = _dot(block, w[:, pl.ds(pl.multiple_of(mine * half, half), half)])


def _add_kernel(ins, outs, mine, *refs):
    came = refs[0][...] if ins == 1 else jnp.concatenate([ref[...] for ref in refs[:ins]], axis=0)
    total = (mine[...].astype(F32) + came.astype(F32)).astype(BF)
    first = 0
    for out in refs[-outs:]:
        out[...] = total[first : first + out.shape[0]]
        first += out.shape[0]


def _vision_kernel(parts, seen, *refs):
    tokens, scale = refs[2 * parts], refs[2 * parts + 1]
    outs, spread = refs[-1 - seen : -1], refs[-1]
    each = 4 // seen
    first = 0
    for mine, came in zip(refs[:parts], refs[parts : 2 * parts]):
        rows = pl.ds(first, mine.shape[0])
        for j in range(spread.shape[0]):
            lanes = pl.ds(j * 128, 128)
            total = mine[:, lanes].astype(F32) + came[:, lanes].astype(F32)
            vision = tokens[rows, lanes].astype(F32) + scale[:, lanes] * total
            spread[j, rows, :] = vision.astype(BF).astype(F32)
        first += mine.shape[0]
    for j in range(spread.shape[0]):
        for k in range(4):
            out = outs[k // each]
            out[k % each, :, pl.ds(j * 128, 128)] = spread[j, pl.ds(k, out.shape[1], stride=4), :].astype(BF)


def _residual_kernel(half, pieces, info, tokens, scale, *refs):
    sems, outs = refs[-1], refs[-2 - len(pieces) : -2]
    lanes = pl.ds(pl.multiple_of(info[0] * half, half), half)
    patches = tokens.shape[0] // 4
    copies = []
    for i, (block, first, count) in enumerate(pieces):
        rows = pl.ds(pl.multiple_of(info[3 + block] * patches + first, 32), count)
        copies.append(pltpu.make_async_copy(tokens.at[rows, lanes], outs[i], sems.at[i]))
        copies[-1].start()
    refs[-2][...] = scale[:, lanes].astype(F32)
    for copy in copies:
        copy.wait()


def _relay_kernel(first, block, *refs):
    refs[-1][...] = block[pl.ds(first, refs[-1].shape[0]), :]


def _hold_kernel(weight, *refs):
    held, sem = refs[-2:]
    copy = pltpu.make_async_copy(weight, held, sem)
    copy.start()
    copy.wait()


def _head_kernel(half, blocks, info, *refs):
    own, weight = refs[:blocks], refs[blocks]
    here = pl.ds(pl.multiple_of(info[0] * half, half), half)
    each = 4 // blocks
    part = None
    for k in range(4):
        more = _dot(own[k // each][k % each], weight[k, here, :])
        part = more if part is None else part + more
    refs[-1][...] = part


def _merge_kernel(half, blocks, late, first, head, info, *refs):
    own, other, weight = refs[:blocks], refs[blocks : 2 * blocks], refs[2 * blocks]
    mine = info[0]
    here = pl.ds(pl.multiple_of(mine * half, half), half)
    there = pl.ds(pl.multiple_of((1 - mine) * half, half), half)

    each = 4 // blocks
    part = refs[2 * blocks + 3][...] if head else None
    for k in range(4):
        i, j = k // each, k % each
        more = _dot(other[i][j], weight[k, there, :])
        if not head:
            more = more + _dot(own[i][j], weight[k, here, :])
        part = more if part is None else part + more
    if late is None:
        refs[-1][...] = part.astype(BF)
        return
    near, next_to = refs[2 * blocks + 1], refs[2 * blocks + 2]
    second = info[1] > 0 if late == 0 else info[1] == 0
    found = pl.ds(first, part.shape[0])
    part = part + jnp.where(second, next_to[found, :], near[found, :]).astype(F32)
    refs[-1][...] = part
    refs[-2][...] = part.astype(BF)


def _hits(info, where_to, first, count, rows):
    index = lax.broadcasted_iota(jnp.int32, (rows, count), 0) + info[3] * rows
    return (index == where_to[:, first : first + count]).astype(F32)


def _early_kernel(parts, late, info, where_to, *refs):
    text, out, spots = refs[parts], refs[-2], refs[-1]
    projected = jnp.concatenate([ref[...] for ref in refs[:parts]], axis=0)
    rows = out.shape[0]
    to_come = _hits(info, where_to, 0, late, rows)
    hit = _hits(info, where_to, late, projected.shape[0], rows)
    image = _dot(hit.astype(BF), projected).astype(BF)
    taken = jnp.max(hit, axis=1, keepdims=True) + jnp.max(to_come, axis=1, keepdims=True)
    out[...] = jnp.where(taken > 0, image, text[...])
    spots[...] = to_come.astype(BF)


def _late_kernel(parts, base, spots, *refs):
    projected = jnp.concatenate([ref[...] for ref in refs[:parts]], axis=0)
    refs[-1][...] = (_dot(spots[...], projected) + base[...].astype(F32)).astype(BF)


def _place_kernel(parts, info, where_to, *refs):
    text, out = refs[parts], refs[-1]
    projected = jnp.concatenate([ref[...] for ref in refs[:parts]], axis=0)
    hit = _hits(info, where_to, 0, projected.shape[0], out.shape[0])
    image = _dot(hit.astype(BF), projected).astype(BF)
    out[...] = jnp.where(jnp.max(hit, axis=1, keepdims=True) > 0, image, text[...])


HBM = pl.BlockSpec(memory_space=pltpu.HBM)
VMEM = pl.BlockSpec(memory_space=pltpu.VMEM)
SMEM = pl.BlockSpec(memory_space=pltpu.SMEM)


def build(rows, cols):
    def swap(x, axis, bit):
        size = rows if axis == "row" else cols
        return lax.ppermute(x, axis, [(i, i ^ bit) for i in range(size)])

    def per_device(hidden, down_weight, tokens, layer_scale, merge_weight, text_embeds, positions):
        patches, depth = hidden.shape
        width = down_weight.shape[1]
        half = width // 2
        merged_rows = patches // 4
        dec = merge_weight.shape[2]
        row, col = lax.axis_index("row"), lax.axis_index("col")
        mine = row % 2
        inner = (col == 1) | (col == 2)
        low = col < 2
        near, far = jnp.where(low, 2, 1), jnp.where(low, 3, 0)
        info = jnp.stack([mine, inner.astype(jnp.int32), 1 - col % 2, col, col ^ 1, near, far])
        scale = layer_scale[None, :]
        row_bits = [1 << i for i in range(1, rows.bit_length() - 1)]
        after = []

        def stay(x):
            return pltpu.with_memory_space_constraint(x, pltpu.VMEM)

        def hold():
            held = pl.pallas_call(
                _hold_kernel,
                out_shape=_near(merge_weight.shape, BF),
                in_specs=[HBM] + [ANY] * len(after),
                out_specs=VMEM,
                scratch_shapes=[pltpu.SemaphoreType.DMA],
                cost_estimate=LITTLE,
                compiler_params=pltpu.CompilerParams(vmem_limit_bytes=ROOM),
                name="hold",
            )(pltpu.with_memory_space_constraint(merge_weight, pltpu.HBM), *after)
            after[:] = [held]
            return held

        def residuals(pieces):
            *copies, own_scale = pl.pallas_call(
                functools.partial(_residual_kernel, half, pieces),
                out_shape=tuple(_near((count, half), BF) for _, _, count in pieces) + (_near((1, half), F32),),
                in_specs=[SMEM, HBM, VMEM] + [ANY] * len(after),
                out_specs=(VMEM,) * (len(pieces) + 1),
                scratch_shapes=[pltpu.SemaphoreType.DMA((len(pieces),))],
                cost_estimate=LITTLE,
                compiler_params=pltpu.CompilerParams(vmem_limit_bytes=ROOM),
                name="residuals",
            )(info, pltpu.with_memory_space_constraint(tokens, pltpu.HBM), scale, *after)
            after[:] = [copies[0]]
            return copies, own_scale

        def relay(block, first, count):
            same = pl.pallas_call(
                functools.partial(_relay_kernel, first),
                out_shape=_near((count, depth), BF),
                in_specs=[VMEM] + [ANY] * len(after),
                out_specs=VMEM,
                cost_estimate=LITTLE,
                compiler_params=pltpu.CompilerParams(vmem_limit_bytes=ROOM),
                name="relay",
            )(block, *after)
            after[:] = [same]
            return same

        def down(*blocks, parts=2, keep=1):
            count = blocks[0].shape[0]
            outs = [_near((count // parts, half), BF)] * parts if parts else []
            outs += [_near((count, half), F32)] * keep
            given = pl.pallas_call(
                functools.partial(_down_kernel, half, len(blocks), (parts, keep)),
                out_shape=tuple(outs),
                in_specs=[SMEM] + [VMEM] * (len(blocks) + 1) + [ANY] * len(after),
                out_specs=(VMEM,) * len(outs),
                cost_estimate=LITTLE,
                compiler_params=pltpu.CompilerParams(vmem_limit_bytes=ROOM),
                name="down",
            )(info, *blocks, down_weight, *after)
            after[:] = [given[0]]
            return tuple(given[:parts]), given[-1]

        def add(total, came, *rows):
            counts = rows or (total.shape[0],)
            came = came if isinstance(came, tuple) else (came,)
            give = pl.pallas_call(
                functools.partial(_add_kernel, len(came), len(counts)),
                out_shape=tuple(_near((n, total.shape[1]), BF) for n in counts),
                in_specs=[VMEM] * (1 + len(came)) + [ANY] * len(after),
                out_specs=tuple(VMEM for _ in counts),
                cost_estimate=LITTLE,
                compiler_params=pltpu.CompilerParams(vmem_limit_bytes=ROOM),
                name="add",
            )(stay(total), *came, *after)
            after[:] = [give[0]]
            return give if rows else give[0]

        def see(mine_parts, came_parts, residual, own_scale, parts=2):
            count = residual.shape[0]
            out = pl.pallas_call(
                functools.partial(_vision_kernel, len(mine_parts), parts),
                out_shape=(_near((4 // parts, count // 4, half), BF),) * parts,
                in_specs=[VMEM] * (2 * len(mine_parts) + 2) + [ANY] * len(after),
                out_specs=(VMEM,) * parts,
                scratch_shapes=[pltpu.VMEM((half // 128, count, 128), F32)],
                cost_estimate=LITTLE,
                compiler_params=pltpu.CompilerParams(vmem_limit_bytes=ROOM),
                name="vision",
            )(*mine_parts, *came_parts, stay(residual), stay(own_scale), *after)
            after[:] = [out[0]]
            return tuple(out)

        def merge_head(own, weight):
            count = own[0].shape[1]
            part = pl.pallas_call(
                functools.partial(_head_kernel, half, len(own)),
                out_shape=_near((count, dec), F32),
                in_specs=[SMEM] + [VMEM] * (len(own) + 1) + [ANY] * len(after),
                out_specs=VMEM,
                cost_estimate=LITTLE,
                compiler_params=pltpu.CompilerParams(vmem_limit_bytes=ROOM),
                name="merge_head",
            )(info, *own, stay(weight), *after)
            after[:] = [part]
            return part

        def merge(own, other, weight, came=None, late=None, first=0, head=None):
            count = own[0].shape[1]
            extra = [] if came is None else list(came)
            extra += [] if head is None else [stay(head)]
            outs = [_near((count, dec), BF)] + [_near((count, dec), F32)] * (came is not None)
            given = pl.pallas_call(
                functools.partial(_merge_kernel, half, len(own), late, first, head is not None),
                out_shape=tuple(outs),
                in_specs=[SMEM] + [VMEM] * (2 * len(own) + 1 + len(extra)) + [ANY] * len(after),
                out_specs=(VMEM,) * len(outs),
                cost_estimate=LITTLE,
                compiler_params=pltpu.CompilerParams(vmem_limit_bytes=ROOM),
                name="merge",
            )(info, *own, *other, stay(weight), *extra, *after)
            after[:] = [given[0]]
            return given[0] if came is None else given

        def place(parts, where_to):
            return pl.pallas_call(
                functools.partial(_place_kernel, len(parts)),
                out_shape=jax.ShapeDtypeStruct(text_embeds.shape, BF),
                in_specs=[SMEM, VMEM] + [VMEM] * (len(parts) + 1) + [ANY] * len(after),
                out_specs=VMEM,
                cost_estimate=LITTLE,
                compiler_params=pltpu.CompilerParams(vmem_limit_bytes=ROOM),
                name="place",
            )(info, where_to, *parts, text_embeds, *after)

        def place_early(parts, late, where_to):
            base, spots = pl.pallas_call(
                functools.partial(_early_kernel, len(parts), late),
                out_shape=(_near(text_embeds.shape, BF), _near((text_embeds.shape[0], late), BF)),
                in_specs=[SMEM, VMEM] + [VMEM] * (len(parts) + 1) + [ANY] * len(after),
                out_specs=(VMEM, VMEM),
                cost_estimate=LITTLE,
                compiler_params=pltpu.CompilerParams(vmem_limit_bytes=ROOM),
                name="place_early",
            )(info, where_to, *parts, text_embeds, *after)
            after[:] = [spots]
            return base, spots

        def place_late(base, spots, parts):
            return pl.pallas_call(
                functools.partial(_late_kernel, len(parts)),
                out_shape=jax.ShapeDtypeStruct(text_embeds.shape, BF),
                in_specs=[VMEM] * (len(parts) + 2) + [ANY] * len(after),
                out_specs=VMEM,
                cost_estimate=LITTLE,
                compiler_params=pltpu.CompilerParams(vmem_limit_bytes=ROOM),
                name="place_late",
            )(stay(base), stay(spots), *parts, *after)

        if cols != 4:
            held = hold()
            parts = jnp.zeros((cols * merged_rows, dec), F32)
            for step in range(cols):
                block = hidden if step == 0 else swap(hidden, "col", step)
                owner = jnp.bitwise_xor(col, step)
                give, total = down(block)
                came = tuple(swap(part, "row", 1) for part in give)
                for bit in row_bits:
                    total = add(total, came)
                    came = swap(total, "row", bit)
                residual = lax.dynamic_slice(tokens, (owner * patches, mine * half), (patches, half))
                own_scale = lax.dynamic_slice(scale, (0, mine * half), (1, half)).astype(F32)
                own = see([total], [came], residual, own_scale)
                part = merge(own, tuple(swap(v, "row", 1) for v in own), held).astype(F32)
                parts = lax.dynamic_update_slice(parts, part, (owner * merged_rows, 0))
            return place([lax.psum(parts, "col").astype(BF)], positions[None, :])

        between, outward = [(1, 2), (2, 1)], [(1, 0), (2, 3)]
        bit_x, bit_y = (row_bits + row_bits)[:2] if row_bits else (1, 1)

        def x(give):
            return swap(give, "row", bit_x)

        def y(give):
            return swap(give, "row", bit_y)

        def core(parts):
            return tuple(swap(part, "row", 1) for part in parts)

        def pairs(give):
            return swap(give, "col", 1)

        def halves(give):
            return swap(give, "col", 2)

        at = [positions[i * merged_rows : (i + 1) * merged_rows] for i in range(4)]
        where_to = jnp.concatenate(
            [
                jnp.where(low, at[1], at[2]),
                jnp.where(low, at[0], at[3]),
                jnp.where(low, at[2], at[1]),
                jnp.where(low, at[3], at[0]),
            ]
        )[None, :]
        after.extend([scale, where_to])
        pieces = [(i, 0, patches) for i in range(4)]
        last = len(pieces)
        v = {}
        v["hop_a"] = swap(hidden, "col", 1)
        v["hop_b"] = lax.ppermute(hidden, "col", between)
        v["hop_c"] = lax.ppermute(v["hop_b"], "col", outward)
        v["hop_d"] = lax.ppermute(v["hop_a"], "col", between)

        def send_on(i):
            v["mid", i] = relay(v["hop_d"], *pieces[i][1:])
            v["hop", i] = lax.ppermute(v["mid", i], "col", outward)

        def send_down(i):
            if i < 3:
                blocks = [[hidden], [v["hop_a"]], [v["hop_b"], v["hop_c"]]][i]
            else:
                blocks = [v["mid", i], v["hop", i]]
            v["block", i] = blocks
            give, v["keep", i] = down(*blocks, parts=PARTS[i], keep=0 if f"keep{i}" in ORDER else 1)
            v["core", i] = core(give)

        def stay_down(i):
            _, v["keep", i] = down(*v["block", i], parts=0)

        def first_sum(i):
            if i in SPLIT:
                count = pieces[i][2]
                v["sum", i] = add(v["keep", i], v["core", i], count // 2, count // 2)
                v["in", i] = [x(v["sum", i][0]), y(v["sum", i][1])]
            else:
                v["sum", i] = [add(v["keep", i], v["core", i])]
                v["in", i] = [x(v["sum", i][0])]
            v["turn", i], v["back", i] = [], []

        def second_sum(i):
            j = len(v["turn", i])
            v["turn", i].append(add(v["sum", i][j], v["in", i][j]))
            v["back", i].append((x if j else y)(v["turn", i][j]))

        def look(i):
            seen = see(v["turn", i], v["back", i], v["residual"][i], v["scale"], SEEN[i])
            v["seen", i], v["other", i] = seen, core(seen)

        def project(i):
            if i < 2:
                v["far", i] = halves(merge(v["seen", i], v["other", i], v["held"]))
            else:
                block, first, _ = pieces[i]
                late = block - 2, first // 4
                give, v["part", i] = merge(v["seen", i], v["other", i], v["held"], (v["far", 0], v["far", 1]), *late, v.get(("head", i)))
                v["pair", i] = pairs(give)

        def project_head(i):
            v["head", i] = merge_head(v["seen", i], v["held"])

        def complete(i):
            v["away", i] = add(v["part", i], v["pair", i])
            v["own", i] = halves(v["away", i])

        def others(name):
            if name == "hold":
                v["held"] = hold()
            elif name == "residual":
                v["residual"], v["scale"] = residuals(pieces)
            elif name == "early":
                v["base"] = place_early([v["away", i] for i in range(2, last)], 2 * merged_rows, where_to)

        calls = {
            "hop": send_on,
            "down": send_down,
            "keep": stay_down,
            "sum": first_sum,
            "turn": second_sum,
            "see": look,
            "merge": project,
            "head": project_head,
            "done": complete,
        }
        for step in ORDER:
            name, _, waits = step.partition(":")
            for wait in waits.split(",") if waits else ():
                after.append(v[wait if wait.startswith("hop_") else (wait[:-1], int(wait[-1]))])
            if name[:-1] in calls:
                calls[name[:-1]](int(name[-1]))
            else:
                others(name)
        return place_late(*v["base"], [v["own", i] for i in range(2, last)])

    return per_device


def solution(mesh):
    in_specs = (
        P("col", "row"),
        P("row", "col"),
        P(None, "col"),
        P("col"),
        P(None, "col", "row"),
        P("col", "row"),
        P(),
    )
    out_specs = P("col", "row")
    return jax.shard_map(
        build(mesh.shape["row"], mesh.shape["col"]),
        mesh=mesh,
        in_specs=in_specs,
        out_specs=out_specs,
        check_vma=False,
    )
```

```python
import functools

import jax
import jax.numpy as jnp
from jax import lax
from jax.experimental import pallas as pl
from jax.experimental.pallas import tpu as pltpu
from jax.sharding import PartitionSpec as P

BF = jnp.bfloat16
F32 = jnp.float32
ANY = pl.BlockSpec(memory_space=pl.ANY)
LITTLE = pl.CostEstimate(flops=1, bytes_accessed=1, transcendentals=0)
ROOM = 8 * 1024 * 1024
PARTS = (2, 2, 2, 2)
SPLIT = (2, 3)
SEEN = (2, 2, 2, 2)
ORDER = (
    "down0", "sum0", "turn0", "down1:hop_b", "sum1", "residual", "hold", "see0",
    "merge0", "hop3", "down2:hop_d", "turn1", "sum2", "see1:far0", "turn2", "turn2",
    "merge1", "down3", "see2", "keep3", "sum3", "turn3:far1", "turn3:far0", "merge2", "see3:pair2",
    "head3", "merge3", "done2", "done3", "early",
)


def _near(shape, kind):
    return pltpu.VMEM(shape, kind)


def _dot(a, b):
    return jnp.dot(a, b, preferred_element_type=F32)


def _down_kernel(half, blocks, parts, info, *refs):
    w, outs = refs[blocks], refs[-parts[0] - parts[1] :]
    mine = info[0]
    block = refs[0][...] if blocks == 1 else jnp.where(info[1] > 0, refs[0][...], refs[1][...])
    if parts[0]:
        give = _dot(block, w[:, pl.ds(pl.multiple_of((1 - mine) * half, half), half)]).astype(BF)
        count = outs[0].shape[0]
        for i, out in enumerate(outs[: parts[0]]):
            out[...] = give[i * count : (i + 1) * count]
    if parts[1]:
        outs[-1][...] = _dot(block, w[:, pl.ds(pl.multiple_of(mine * half, half), half)])


def _add_kernel(ins, outs, mine, *refs):
    came = refs[0][...] if ins == 1 else jnp.concatenate([ref[...] for ref in refs[:ins]], axis=0)
    total = (mine[...].astype(F32) + came.astype(F32)).astype(BF)
    first = 0
    for out in refs[-outs:]:
        out[...] = total[first : first + out.shape[0]]
        first += out.shape[0]


def _vision_kernel(parts, seen, *refs):
    tokens, scale = refs[2 * parts], refs[2 * parts + 1]
    outs, spread = refs[-1 - seen : -1], refs[-1]
    each = 4 // seen
    first = 0
    for mine, came in zip(refs[:parts], refs[parts : 2 * parts]):
        rows = pl.ds(first, mine.shape[0])
        for j in range(spread.shape[0]):
            lanes = pl.ds(j * 128, 128)
            total = mine[:, lanes].astype(F32) + came[:, lanes].astype(F32)
            vision = tokens[rows, lanes].astype(F32) + scale[:, lanes] * total
            spread[j, rows, :] = vision.astype(BF).astype(F32)
        first += mine.shape[0]
    for j in range(spread.shape[0]):
        for k in range(4):
            out = outs[k // each]
            out[k % each, :, pl.ds(j * 128, 128)] = spread[j, pl.ds(k, out.shape[1], stride=4), :].astype(BF)


def _residual_kernel(half, pieces, info, tokens, scale, *refs):
    sems, outs = refs[-1], refs[-2 - len(pieces) : -2]
    lanes = pl.ds(pl.multiple_of(info[0] * half, half), half)
    patches = tokens.shape[0] // 4
    copies = []
    for i, (block, first, count) in enumerate(pieces):
        rows = pl.ds(pl.multiple_of(info[3 + block] * patches + first, 32), count)
        copies.append(pltpu.make_async_copy(tokens.at[rows, lanes], outs[i], sems.at[i]))
        copies[-1].start()
    refs[-2][...] = scale[:, lanes].astype(F32)
    for copy in copies:
        copy.wait()


def _relay_kernel(first, block, *refs):
    refs[-1][...] = block[pl.ds(first, refs[-1].shape[0]), :]


def _hold_kernel(weight, *refs):
    held, sem = refs[-2:]
    copy = pltpu.make_async_copy(weight, held, sem)
    copy.start()
    copy.wait()


def _head_kernel(half, blocks, info, *refs):
    own, weight = refs[:blocks], refs[blocks]
    here = pl.ds(pl.multiple_of(info[0] * half, half), half)
    each = 4 // blocks
    part = None
    for k in range(4):
        more = _dot(own[k // each][k % each], weight[k, here, :])
        part = more if part is None else part + more
    refs[-1][...] = part


def _merge_kernel(half, blocks, late, first, head, info, *refs):
    own, other, weight = refs[:blocks], refs[blocks : 2 * blocks], refs[2 * blocks]
    mine = info[0]
    here = pl.ds(pl.multiple_of(mine * half, half), half)
    there = pl.ds(pl.multiple_of((1 - mine) * half, half), half)

    each = 4 // blocks
    part = refs[2 * blocks + 3][...] if head else None
    for k in range(4):
        i, j = k // each, k % each
        more = _dot(other[i][j], weight[k, there, :])
        if not head:
            more = more + _dot(own[i][j], weight[k, here, :])
        part = more if part is None else part + more
    if late is None:
        refs[-1][...] = part.astype(BF)
        return
    near, next_to = refs[2 * blocks + 1], refs[2 * blocks + 2]
    second = info[1] > 0 if late == 0 else info[1] == 0
    found = pl.ds(first, part.shape[0])
    part = part + jnp.where(second, next_to[found, :], near[found, :]).astype(F32)
    refs[-1][...] = part
    refs[-2][...] = part.astype(BF)


def _hits(info, where_to, first, count, rows):
    index = lax.broadcasted_iota(jnp.int32, (rows, count), 0) + info[3] * rows
    return (index == where_to[:, first : first + count]).astype(F32)


def _early_kernel(parts, late, info, where_to, *refs):
    text, out, spots = refs[parts], refs[-2], refs[-1]
    projected = jnp.concatenate([ref[...] for ref in refs[:parts]], axis=0)
    rows = out.shape[0]
    to_come = _hits(info, where_to, 0, late, rows)
    hit = _hits(info, where_to, late, projected.shape[0], rows)
    image = _dot(hit.astype(BF), projected).astype(BF)
    taken = jnp.max(hit, axis=1, keepdims=True) + jnp.max(to_come, axis=1, keepdims=True)
    out[...] = jnp.where(taken > 0, image, text[...])
    spots[...] = to_come.astype(BF)


def _late_kernel(parts, base, spots, *refs):
    projected = jnp.concatenate([ref[...] for ref in refs[:parts]], axis=0)
    refs[-1][...] = (_dot(spots[...], projected) + base[...].astype(F32)).astype(BF)


def _place_kernel(parts, info, where_to, *refs):
    text, out = refs[parts], refs[-1]
    projected = jnp.concatenate([ref[...] for ref in refs[:parts]], axis=0)
    hit = _hits(info, where_to, 0, projected.shape[0], out.shape[0])
    image = _dot(hit.astype(BF), projected).astype(BF)
    out[...] = jnp.where(jnp.max(hit, axis=1, keepdims=True) > 0, image, text[...])


HBM = pl.BlockSpec(memory_space=pltpu.HBM)
VMEM = pl.BlockSpec(memory_space=pltpu.VMEM)
SMEM = pl.BlockSpec(memory_space=pltpu.SMEM)


def build(rows, cols):
    def swap(x, axis, bit):
        size = rows if axis == "row" else cols
        return lax.ppermute(x, axis, [(i, i ^ bit) for i in range(size)])

    def per_device(hidden, down_weight, tokens, layer_scale, merge_weight, text_embeds, positions):
        patches, depth = hidden.shape
        width = down_weight.shape[1]
        half = width // 2
        merged_rows = patches // 4
        dec = merge_weight.shape[2]
        row, col = lax.axis_index("row"), lax.axis_index("col")
        mine = row % 2
        inner = (col == 1) | (col == 2)
        low = col < 2
        near, far = jnp.where(low, 2, 1), jnp.where(low, 3, 0)
        info = jnp.stack([mine, inner.astype(jnp.int32), 1 - col % 2, col, col ^ 1, near, far])
        scale = layer_scale[None, :]
        row_bits = [1 << i for i in range(1, rows.bit_length() - 1)]
        after = []

        def stay(x):
            return pltpu.with_memory_space_constraint(x, pltpu.VMEM)

        def hold():
            held = pl.pallas_call(
                _hold_kernel,
                out_shape=_near(merge_weight.shape, BF),
                in_specs=[HBM] + [ANY] * len(after),
                out_specs=VMEM,
                scratch_shapes=[pltpu.SemaphoreType.DMA],
                cost_estimate=LITTLE,
                compiler_params=pltpu.CompilerParams(vmem_limit_bytes=ROOM),
                name="hold",
            )(pltpu.with_memory_space_constraint(merge_weight, pltpu.HBM), *after)
            after[:] = [held]
            return held

        def residuals(pieces):
            *copies, own_scale = pl.pallas_call(
                functools.partial(_residual_kernel, half, pieces),
                out_shape=tuple(_near((count, half), BF) for _, _, count in pieces) + (_near((1, half), F32),),
                in_specs=[SMEM, HBM, VMEM] + [ANY] * len(after),
                out_specs=(VMEM,) * (len(pieces) + 1),
                scratch_shapes=[pltpu.SemaphoreType.DMA((len(pieces),))],
                cost_estimate=LITTLE,
                compiler_params=pltpu.CompilerParams(vmem_limit_bytes=ROOM),
                name="residuals",
            )(info, pltpu.with_memory_space_constraint(tokens, pltpu.HBM), scale, *after)
            after[:] = [copies[0]]
            return copies, own_scale

        def relay(block, first, count):
            same = pl.pallas_call(
                functools.partial(_relay_kernel, first),
                out_shape=_near((count, depth), BF),
                in_specs=[VMEM] + [ANY] * len(after),
                out_specs=VMEM,
                cost_estimate=LITTLE,
                compiler_params=pltpu.CompilerParams(vmem_limit_bytes=ROOM),
                name="relay",
            )(block, *after)
            after[:] = [same]
            return same

        def down(*blocks, parts=2, keep=1):
            count = blocks[0].shape[0]
            outs = [_near((count // parts, half), BF)] * parts if parts else []
            outs += [_near((count, half), F32)] * keep
            given = pl.pallas_call(
                functools.partial(_down_kernel, half, len(blocks), (parts, keep)),
                out_shape=tuple(outs),
                in_specs=[SMEM] + [VMEM] * (len(blocks) + 1) + [ANY] * len(after),
                out_specs=(VMEM,) * len(outs),
                cost_estimate=LITTLE,
                compiler_params=pltpu.CompilerParams(vmem_limit_bytes=ROOM),
                name="down",
            )(info, *blocks, down_weight, *after)
            after[:] = [given[0]]
            return tuple(given[:parts]), given[-1]

        def add(total, came, *rows):
            counts = rows or (total.shape[0],)
            came = came if isinstance(came, tuple) else (came,)
            give = pl.pallas_call(
                functools.partial(_add_kernel, len(came), len(counts)),
                out_shape=tuple(_near((n, total.shape[1]), BF) for n in counts),
                in_specs=[VMEM] * (1 + len(came)) + [ANY] * len(after),
                out_specs=tuple(VMEM for _ in counts),
                cost_estimate=LITTLE,
                compiler_params=pltpu.CompilerParams(vmem_limit_bytes=ROOM),
                name="add",
            )(stay(total), *came, *after)
            after[:] = [give[0]]
            return give if rows else give[0]

        def see(mine_parts, came_parts, residual, own_scale, parts=2):
            count = residual.shape[0]
            out = pl.pallas_call(
                functools.partial(_vision_kernel, len(mine_parts), parts),
                out_shape=(_near((4 // parts, count // 4, half), BF),) * parts,
                in_specs=[VMEM] * (2 * len(mine_parts) + 2) + [ANY] * len(after),
                out_specs=(VMEM,) * parts,
                scratch_shapes=[pltpu.VMEM((half // 128, count, 128), F32)],
                cost_estimate=LITTLE,
                compiler_params=pltpu.CompilerParams(vmem_limit_bytes=ROOM),
                name="vision",
            )(*mine_parts, *came_parts, stay(residual), stay(own_scale), *after)
            after[:] = [out[0]]
            return tuple(out)

        def merge_head(own, weight):
            count = own[0].shape[1]
            part = pl.pallas_call(
                functools.partial(_head_kernel, half, len(own)),
                out_shape=_near((count, dec), F32),
                in_specs=[SMEM] + [VMEM] * (len(own) + 1) + [ANY] * len(after),
                out_specs=VMEM,
                cost_estimate=LITTLE,
                compiler_params=pltpu.CompilerParams(vmem_limit_bytes=ROOM),
                name="merge_head",
            )(info, *own, stay(weight), *after)
            after[:] = [part]
            return part

        def merge(own, other, weight, came=None, late=None, first=0, head=None):
            count = own[0].shape[1]
            extra = [] if came is None else list(came)
            extra += [] if head is None else [stay(head)]
            outs = [_near((count, dec), BF)] + [_near((count, dec), F32)] * (came is not None)
            given = pl.pallas_call(
                functools.partial(_merge_kernel, half, len(own), late, first, head is not None),
                out_shape=tuple(outs),
                in_specs=[SMEM] + [VMEM] * (2 * len(own) + 1 + len(extra)) + [ANY] * len(after),
                out_specs=(VMEM,) * len(outs),
                cost_estimate=LITTLE,
                compiler_params=pltpu.CompilerParams(vmem_limit_bytes=ROOM),
                name="merge",
            )(info, *own, *other, stay(weight), *extra, *after)
            after[:] = [given[0]]
            return given[0] if came is None else given

        def place(parts, where_to):
            return pl.pallas_call(
                functools.partial(_place_kernel, len(parts)),
                out_shape=jax.ShapeDtypeStruct(text_embeds.shape, BF),
                in_specs=[SMEM, VMEM] + [VMEM] * (len(parts) + 1) + [ANY] * len(after),
                out_specs=VMEM,
                cost_estimate=LITTLE,
                compiler_params=pltpu.CompilerParams(vmem_limit_bytes=ROOM),
                name="place",
            )(info, where_to, *parts, text_embeds, *after)

        def place_early(parts, late, where_to):
            base, spots = pl.pallas_call(
                functools.partial(_early_kernel, len(parts), late),
                out_shape=(_near(text_embeds.shape, BF), _near((text_embeds.shape[0], late), BF)),
                in_specs=[SMEM, VMEM] + [VMEM] * (len(parts) + 1) + [ANY] * len(after),
                out_specs=(VMEM, VMEM),
                cost_estimate=LITTLE,
                compiler_params=pltpu.CompilerParams(vmem_limit_bytes=ROOM),
                name="place_early",
            )(info, where_to, *parts, text_embeds, *after)
            after[:] = [spots]
            return base, spots

        def place_late(base, spots, parts):
            return pl.pallas_call(
                functools.partial(_late_kernel, len(parts)),
                out_shape=jax.ShapeDtypeStruct(text_embeds.shape, BF),
                in_specs=[VMEM] * (len(parts) + 2) + [ANY] * len(after),
                out_specs=VMEM,
                cost_estimate=LITTLE,
                compiler_params=pltpu.CompilerParams(vmem_limit_bytes=ROOM),
                name="place_late",
            )(stay(base), stay(spots), *parts, *after)

        if cols != 4:
            held = hold()
            parts = jnp.zeros((cols * merged_rows, dec), F32)
            for step in range(cols):
                block = hidden if step == 0 else swap(hidden, "col", step)
                owner = jnp.bitwise_xor(col, step)
                give, total = down(block)
                came = tuple(swap(part, "row", 1) for part in give)
                for bit in row_bits:
                    total = add(total, came)
                    came = swap(total, "row", bit)
                residual = lax.dynamic_slice(tokens, (owner * patches, mine * half), (patches, half))
                own_scale = lax.dynamic_slice(scale, (0, mine * half), (1, half)).astype(F32)
                own = see([total], [came], residual, own_scale)
                part = merge(own, tuple(swap(v, "row", 1) for v in own), held).astype(F32)
                parts = lax.dynamic_update_slice(parts, part, (owner * merged_rows, 0))
            return place([lax.psum(parts, "col").astype(BF)], positions[None, :])

        between, outward = [(1, 2), (2, 1)], [(1, 0), (2, 3)]
        bit_x, bit_y = (row_bits + row_bits)[:2] if row_bits else (1, 1)

        def x(give):
            return swap(give, "row", bit_x)

        def y(give):
            return swap(give, "row", bit_y)

        def core(parts):
            return tuple(swap(part, "row", 1) for part in parts)

        def pairs(give):
            return swap(give, "col", 1)

        def halves(give):
            return swap(give, "col", 2)

        at = [positions[i * merged_rows : (i + 1) * merged_rows] for i in range(4)]
        where_to = jnp.concatenate(
            [
                jnp.where(low, at[1], at[2]),
                jnp.where(low, at[0], at[3]),
                jnp.where(low, at[2], at[1]),
                jnp.where(low, at[3], at[0]),
            ]
        )[None, :]
        after.extend([scale, where_to])
        pieces = [(i, 0, patches) for i in range(4)]
        last = len(pieces)
        v = {}
        v["hop_a"] = swap(hidden, "col", 1)
        v["hop_b"] = lax.ppermute(hidden, "col", between)
        v["hop_c"] = lax.ppermute(v["hop_b"], "col", outward)
        v["hop_d"] = lax.ppermute(v["hop_a"], "col", between)

        def send_on(i):
            v["mid", i] = relay(v["hop_d"], *pieces[i][1:])
            v["hop", i] = lax.ppermute(v["mid", i], "col", outward)

        def send_down(i):
            if i < 3:
                blocks = [[hidden], [v["hop_a"]], [v["hop_b"], v["hop_c"]]][i]
            else:
                blocks = [v["mid", i], v["hop", i]]
            v["block", i] = blocks
            give, v["keep", i] = down(*blocks, parts=PARTS[i], keep=0 if f"keep{i}" in ORDER else 1)
            v["core", i] = core(give)

        def stay_down(i):
            _, v["keep", i] = down(*v["block", i], parts=0)

        def first_sum(i):
            if i in SPLIT:
                count = pieces[i][2]
                v["sum", i] = add(v["keep", i], v["core", i], count // 2, count // 2)
                v["in", i] = [x(v["sum", i][0]), y(v["sum", i][1])]
            else:
                v["sum", i] = [add(v["keep", i], v["core", i])]
                v["in", i] = [x(v["sum", i][0])]
            v["turn", i], v["back", i] = [], []

        def second_sum(i):
            j = len(v["turn", i])
            v["turn", i].append(add(v["sum", i][j], v["in", i][j]))
            v["back", i].append((x if j else y)(v["turn", i][j]))

        def look(i):
            seen = see(v["turn", i], v["back", i], v["residual"][i], v["scale"], SEEN[i])
            v["seen", i], v["other", i] = seen, core(seen)

        def project(i):
            if i < 2:
                v["far", i] = halves(merge(v["seen", i], v["other", i], v["held"]))
            else:
                block, first, _ = pieces[i]
                late = block - 2, first // 4
                give, v["part", i] = merge(v["seen", i], v["other", i], v["held"], (v["far", 0], v["far", 1]), *late, v.get(("head", i)))
                v["pair", i] = pairs(give)

        def project_head(i):
            v["head", i] = merge_head(v["seen", i], v["held"])

        def complete(i):
            v["away", i] = add(v["part", i], v["pair", i])
            v["own", i] = halves(v["away", i])

        def others(name):
            if name == "hold":
                v["held"] = hold()
            elif name == "residual":
                v["residual"], v["scale"] = residuals(pieces)
            elif name == "early":
                v["base"] = place_early([v["away", i] for i in range(2, last)], 2 * merged_rows, where_to)

        calls = {
            "hop": send_on,
            "down": send_down,
            "keep": stay_down,
            "sum": first_sum,
            "turn": second_sum,
            "see": look,
            "merge": project,
            "head": project_head,
            "done": complete,
        }
        for step in ORDER:
            name, _, waits = step.partition(":")
            for wait in waits.split(",") if waits else ():
                after.append(v[wait if wait.startswith("hop_") else (wait[:-1], int(wait[-1]))])
            if name[:-1] in calls:
                calls[name[:-1]](int(name[-1]))
            else:
                others(name)
        return place_late(*v["base"], [v["own", i] for i in range(2, last)])

    return per_device


def solution(mesh):
    in_specs = (
        P("col", "row"),
        P("row", "col"),
        P(None, "col"),
        P("col"),
        P(None, "col", "row"),
        P("col", "row"),
        P(),
    )
    out_specs = P("col", "row")
    return jax.shard_map(
        build(mesh.shape["row"], mesh.shape["col"]),
        mesh=mesh,
        in_specs=in_specs,
        out_specs=out_specs,
        check_vma=False,
    )
```
